512 devices in a mesh: depth: 32 (over z, y_hi), row: 4 (over y_lo, core), col: 4 (over x).
Axes of the slice: x: 4, y: 8 (y_hi: 4, y_lo: 2; y = y_hi * 2 + y_lo), z: 8, core: 2. Of those that a mesh axis runs over, the one named last changes fastest.
Arguments:
- env_desc: float32 [16384, 1024], P(('depth', 'col')), may hold values from -2.5 to 2.5
- sparse_desc: float32 [4096, 1024], P('row'), may hold values from -2.5 to 2.5
Outputs:
- gram: float32 [4096, 4096], P(('row', 'depth'), 'col')
The draws below stay inside these ranges and needn't reach their ends.
All inputs are finite; a program needn't handle non-finite values.
Results may differ from the reference program's by a relative error of at most 0.00012.
Values sent between devices are 32-bit elements; how exact they have to be, the bound alone decides.
A program may use at most 64 MiB of HBM per device.

```python
import jax
import jax.numpy as jnp
from jax import lax

D = 1024
SPARSE = 4096
N_ENV = 16384


def levels(stream_key, shape, split, smallest, top_value):
    factor_of = 1.0
    for axis_at, shards_of in split:
        steps = jax.random.uniform(jax.random.fold_in(jax.random.fold_in(stream_key, 6), axis_at), (shards_of,), jnp.float32, smallest / len(split), top_value / len(split))
        factor_of = factor_of * jnp.repeat(jnp.exp(steps), shape[axis_at] // shards_of).reshape((-1,) + (1,) * (len(shape) - 1 - axis_at))
    return factor_of


def centred(rng, dims, spread, limit, split=(), held_as=jnp.bfloat16):
    values = spread * jax.random.normal(rng, dims, jnp.float32)
    if split:
        values = values * levels(rng, dims, split, -0.22, 0.18)
    return jnp.clip(values, -limit, limit).astype(held_as)


def setup_inputs(seed: int = 0) -> dict:
    splits = jax.random.split(jax.random.key(seed), 3)
    return {
        "env_desc": centred(splits[0], (N_ENV, D), (1.0 / D ** 0.25), 2.5, ((0, 128),), jnp.float32),
        "sparse_desc": centred(splits[1], (SPARSE, D), (1.0 / D ** 0.25), 2.5, ((0, 4),), jnp.float32),
    }


def reference(env_desc, sparse_desc):
    dots = lax.dot_general(env_desc, sparse_desc, (((1,), (1,)), ((), ())), precision=lax.Precision.HIGHEST, preferred_element_type=jnp.float32)
    squared = dots * dots
    kernel = squared * squared
    total = lax.dot_general(kernel, kernel, (((0,), (0,)), ((), ())), precision=lax.Precision.HIGHEST, preferred_element_type=jnp.float32)
    return total / jnp.float32(N_ENV)
```

```python
import functools

import jax
import jax.numpy as jnp
from jax import lax
from jax.experimental import pallas as pl
from jax.experimental.pallas import tpu as pltpu
from jax.sharding import PartitionSpec as P

MESH = pl.DeviceIdType.MESH
NZ, NY, NX = 8, 4, 4
ENV = 128
PTS = 1024
BLK = 256
NT = (((1,), (1,)), ((), ()))
F32, BF16 = jnp.float32, jnp.bfloat16


def nt(a, b):
    return lax.dot_general(a, b, NT, preferred_element_type=F32)


def halves(v):
    hi = v.astype(BF16)
    return hi, (v - hi.astype(F32)).astype(BF16)


def body(scale, env_ref, sp_ref, out_ref, sf, shi, slo, eg, ec, kf, khi, klo, kx,
         jhi, jlo, tt, zr, yr, zt, yt, fr, fin, tp, tr, loc, ssem, rsem):
    d, r, x = lax.axis_index("depth"), lax.axis_index("row"), lax.axis_index("col")
    z, y, core, yl = d // NY, d % NY, r % 2, r // 2
    sib = r + 1 - 2 * core
    mate = (r + 2) * (1 - yl) + (3 - r) * yl
    user = (3 - r) * (1 - yl) + (r - 2) * yl
    right, left = (x + 1) % NX, (x + NX - 1) % NX

    def at_x(c):
        return (d, r, c)

    def at_row(q):
        return (d, q, x)

    def at_z(k):
        return (((z + k) % NZ) * NY + y, r, x)

    def at_y(k):
        return (z * NY + (y + k) % NY, r, x)

    count = [0, 0]
    sends = []

    def new_recv():
        count[1] += 1
        return count[1] - 1

    def send(src, dst, to, dev):
        c = pltpu.make_async_remote_copy(
            src_ref=src, dst_ref=dst, send_sem=ssem.at[count[0]],
            recv_sem=rsem.at[to], device_id=dev, device_id_type=MESH)
        count[0] += 1
        c.start()
        sends.append(c)

    def arrived(ref, sem):
        pltpu.make_async_copy(ref, ref, rsem.at[sem]).wait()

    load_e = pltpu.make_async_copy(env_ref, eg.at[0], loc.at[0])
    load_e.start()
    loads = []
    for i in range(4):
        rows = pl.ds(i * 256, 256)
        c = pltpu.make_async_copy(sp_ref.at[rows], sf.at[rows], loc.at[1 + i])
        c.start()
        loads.append(c)

    bar = pltpu.get_barrier_semaphore()

    def greet(dev):
        pl.semaphore_signal(bar, inc=1, device_id=dev, device_id_type=MESH)

    for k in range(1, NX):
        greet(at_x((x + k) % NX))
    greet(at_row(sib))
    greet(at_row(mate))
    for k in range(1, NZ):
        greet(at_z(k))
    for k in range(1, NY):
        greet(at_y(k))

    @pl.when(x == user)
    def _():
        def one(i, c):
            greet((i, user, d // 8))
            return c
        lax.fori_loop(0, NZ * NY, one, 0)

    pl.semaphore_wait(bar, 3 + 2 + 7 + 3 + 8)

    def piece(slot, half, p):
        return eg.at[slot, pl.ds(pl.multiple_of(half * 64 + p * 32, 32), 32)]

    def own(p):
        return env_ref.at[pl.ds(pl.multiple_of(core * 64 + p * 32, 32), 32)]

    ring = {(s, p): new_recv() for s in (1, 2, 3) for p in (0, 1)}
    pair = {(s, p): new_recv() for s in (1, 2, 3) for p in (0, 1)}
    send(own(0), piece(1, core, 0), ring[1, 0], at_x(right))
    send(own(1), piece(2, core, 1), ring[2, 1], at_x(left))
    send(own(1), piece(1, core, 1), ring[1, 1], at_x(right))
    send(own(0), piece(2, core, 0), ring[2, 0], at_x(left))

    def to_sib(s, p):
        send(piece(s, core, p), piece(s, core, p), pair[s, p], at_row(sib))

    for i in range(4):
        loads[i].wait()

        @pl.loop(0, 4)
        def _(j):
            rows = pl.ds(pl.multiple_of(i * 256 + j * 64, 64), 64)
            hi, lo = halves(sf[rows])
            shi[rows] = hi
            slo[rows] = lo

    load_e.wait()

    mine = pl.ds(pl.multiple_of(x * BLK, BLK), BLK)
    krecv = {(w, s): new_recv() for w in (0, 1) for s in range(4)}

    def shard(s):
        hi, lo = halves(eg[s])
        ec[0:ENV] = hi
        ec[ENV:] = lo
        cols = slice(s * ENV, (s + 1) * ENV)

        @pl.loop(0, 4)
        def _(i):
            rows = pl.ds(pl.multiple_of(i * 256, 256), 256)
            both = nt(shi[rows], ec[...])
            low = nt(slo[rows], ec[0:ENV])
            dots = both[:, :ENV] + (both[:, ENV:] + low)
            sq = dots * dots
            k = sq * sq
            kf[s, rows] = k
            a, b = halves(k)
            khi[rows, cols] = a
            klo[rows, cols] = b

        send(kf.at[s, mine], kx.at[0, s], krecv[0, s], at_row(sib))
        send(kf.at[s, mine], kx.at[1, s], krecv[1, s], at_row(user))

    arrived(piece(1, core, 0), ring[1, 0])
    send(piece(1, core, 0), piece(3, core, 0), ring[3, 0], at_x(right))
    to_sib(1, 0)
    arrived(piece(2, core, 1), ring[2, 1])
    send(piece(2, core, 1), piece(3, core, 1), ring[3, 1], at_x(left))
    to_sib(2, 1)
    shard(0)
    arrived(piece(1, core, 1), ring[1, 1])
    to_sib(1, 1)
    arrived(piece(2, core, 0), ring[2, 0])
    to_sib(2, 0)
    arrived(piece(1, 1 - core, 0), pair[1, 0])
    arrived(piece(1, 1 - core, 1), pair[1, 1])
    shard(1)
    arrived(piece(3, core, 0), ring[3, 0])
    to_sib(3, 0)
    arrived(piece(3, core, 1), ring[3, 1])
    to_sib(3, 1)
    arrived(piece(2, 1 - core, 1), pair[2, 1])
    arrived(piece(2, 1 - core, 0), pair[2, 0])
    shard(2)
    arrived(piece(3, 1 - core, 0), pair[3, 0])
    arrived(piece(3, 1 - core, 1), pair[3, 1])
    shard(3)

    zring = {(b, t): new_recv() for b in range(4) for t in range(NZ - 1)}
    yring = {(b, t): new_recv() for b in (4, 5) for t in range(NY - 1)}

    def ahead(b):
        return 1 - 2 * (b % 2)

    def zchunk(b, t):
        return (z + 2 * NZ - ahead(b) * (1 + t)) % NZ

    def ychunk(b, t):
        c = (y + 2 * NY - ahead(b) * (1 + t)) % NY
        return pl.ds(pl.multiple_of(c * 32, 32), 32)

    def zsend(b, t):
        send(tt.at[b, zchunk(b, t)], zr.at[b, t], zring[b, t], at_z(ahead(b) % NZ))

    def ysend(b, t):
        send(tt.at[b, :, ychunk(b, t)], yr.at[b - 4, t], yring[b, t], at_y(ahead(b) % NY))

    def gram(p, rhi, rlo):
        @pl.loop(0, 4)
        def _(i):
            rows = pl.ds(pl.multiple_of(i * 256, 256), 256)
            a = khi[rows]
            g = nt(a, rhi) + (nt(a, rlo) + nt(klo[rows], rhi))
            for h in range(2):
                for q in range(2):
                    tt[2 * p + h, 2 * i + q] = g[q * 128:(q + 1) * 128, h * 128:(h + 1) * 128]

    gram(0, khi[mine], klo[mine])
    zsend(0, 0)
    zsend(1, 0)
    for w in (0, 1):
        for s in range(4):
            arrived(kx.at[w, s], krecv[w, s])
            hi, lo = halves(kx[w, s])
            jhi[w, :, s * ENV:(s + 1) * ENV] = hi
            jlo[w, :, s * ENV:(s + 1) * ENV] = lo
        gram(1 + w, jhi[w], jlo[w])
        if w == 0:
            zsend(2, 0)
            zsend(3, 0)
        else:
            ysend(4, 0)
            ysend(5, 0)

    def zstep(t):
        for b in range(4):
            arrived(zr.at[b, t], zring[b, t])
            c = zchunk(b, t + 1)
            tt[b, c] = tt[b, c] + zr[b, t]
            if t < NZ - 2:
                zsend(b, t + 1)

    def ystep(t):
        for b in (4, 5):
            arrived(yr.at[b - 4, t], yring[b, t])
            c = ychunk(b, t + 1)
            tt[b, :, c] = tt[b, :, c] + yr[b - 4, t]
            if t < NY - 2:
                ysend(b, t + 1)

    ztail = {(b, k): new_recv() for b in (4, 5) for k in range(1, NZ)}
    ytail = {(b, k): new_recv() for b in range(4) for k in range(1, NY)}
    own_y = pl.ds(pl.multiple_of(y * 32, 32), 32)
    zstep(0)
    zstep(1)
    ystep(0)
    zstep(2)
    zstep(3)
    ystep(1)
    zstep(4)
    zstep(5)
    ystep(2)
    for k in range(1, NZ):
        for b in (4, 5):
            send(tt.at[b, (z + k) % NZ, own_y], zt.at[b - 4, k - 1], ztail[b, k], at_z(k))
    zstep(6)
    for k in range(1, NY):
        for b in range(4):
            c = pl.ds(pl.multiple_of(((y + k) % NY) * 32, 32), 32)
            send(tt.at[b, z, c], yt.at[b, k - 1], ytail[b, k], at_y(k))

    last = new_recv()

    lane = lax.broadcasted_iota(jnp.int32, (8, 128), 1) // 32
    for b in (4, 5):
        v = tt[b, z, own_y]
        for k in range(1, NZ):
            arrived(zt.at[b - 4, k - 1], ztail[b, k])
            v = v + zt[b - 4, k - 1]
        fr[b] = v * scale
    pad = jnp.zeros((64, 128), F32)
    turned = jnp.concatenate([fr[4], fr[5], pad], axis=0).T
    for h in range(2):
        for q in range(4):
            v = jnp.zeros((8, 128), F32)
            for g in range(4):
                rows = turned[q * 32 + g * 8:q * 32 + g * 8 + 8]
                turn = (g * 32 - h * 32) % 128
                v = jnp.where(lane == g, pltpu.roll(rows, turn, 1) if turn else rows, v)
            tp[h, q] = v
            send(tp.at[h, q], tr.at[d], last, (8 * x + 4 * h + q, mate, r))

    final = []

    def place(p):
        to = (r, sib, mate)[p]
        for h in range(2):
            b = 2 * p + h
            cols = pl.ds(pl.multiple_of(x * BLK + h * 128, 128), 128)
            c = pltpu.make_async_remote_copy(
                src_ref=fr.at[b], dst_ref=fin.at[:, cols], send_sem=ssem.at[count[0]],
                recv_sem=rsem.at[last], device_id=at_x(to), device_id_type=MESH)
            count[0] += 1
            final.append((to, c))

            @pl.when(x == to)
            def _():
                fin[:, cols] = fr[b]

            @pl.when(x != to)
            def _():
                c.start()

    place(2)
    for p in (0, 1):
        for b in (2 * p, 2 * p + 1):
            v = tt[b, z, own_y]
            for k in range(1, NY):
                arrived(yt.at[b, k - 1], ytail[b, k])
                v = v + yt[b, k - 1]
            fr[b] = v * scale
        place(p)

    @pl.when(x != user)
    def _():
        arrived(fin.at[:, 0:768], last)
        out_ref[...] = fin[...]

    @pl.when(x == user)
    def _():
        arrived(tr, last)
        for zz in range(NZ):
            for g in range(4):
                v = jnp.zeros((8, 128), F32)
                for yy in range(NY):
                    rows = tr[zz * NY + yy]
                    turn = ((yy - g) * 32) % 128
                    v = jnp.where(lane == yy, pltpu.roll(rows, turn, 1) if turn else rows, v)
                out_ref[g * 8:g * 8 + 8, zz * 128:(zz + 1) * 128] = v

    for c in sends:
        c.wait_send()
    for to, c in final:
        @pl.when(x != to)
        def _():
            c.wait_send()


def per_device(total, env_desc, sparse_desc):
    vm = pltpu.VMEM
    width = env_desc.shape[1]
    return pl.pallas_call(
        functools.partial(body, 1.0 / total),
        out_shape=jax.ShapeDtypeStruct((32, PTS), F32),
        in_specs=[pl.BlockSpec(memory_space=pl.ANY)] * 2,
        out_specs=pl.BlockSpec(memory_space=pltpu.VMEM),
        scratch_shapes=[
            vm((PTS, width), F32), vm((PTS, width), BF16), vm((PTS, width), BF16),
            vm((4, ENV, width), F32), vm((2 * ENV, width), BF16),
            vm((4, PTS, ENV), F32), vm((PTS, 4 * ENV), BF16), vm((PTS, 4 * ENV), BF16),
            vm((2, 4, BLK, ENV), F32),
            vm((2, BLK, 4 * ENV), BF16), vm((2, BLK, 4 * ENV), BF16),
            vm((6, NZ, 128, 128), F32),
            vm((4, NZ - 1, 128, 128), F32), vm((2, NY - 1, NZ, 32, 128), F32),
            vm((2, NZ - 1, 32, 128), F32), vm((4, NY - 1, 32, 128), F32),
            vm((6, 32, 128), F32), vm((32, PTS), F32),
            vm((2, 4, 8, 128), F32), vm((NZ * NY, 8, 128), F32),
            pltpu.SemaphoreType.DMA((5,)),
            pltpu.SemaphoreType.DMA((100,)),
            pltpu.SemaphoreType.DMA((82,)),
        ],
        compiler_params=pltpu.CompilerParams(
            collective_id=0, has_side_effects=True, vmem_limit_bytes=48 * 2 ** 20),
        cost_estimate=pl.CostEstimate(
            flops=6 * 4 * ENV * PTS * (width + 768), bytes_accessed=5 * 2 ** 20, transcendentals=0),
    )(env_desc, sparse_desc)


def solution(mesh):
    total = ENV * mesh.shape["depth"] * mesh.shape["col"]
    return jax.shard_map(
        functools.partial(per_device, total),
        mesh=mesh,
        in_specs=(P(("depth", "col"), None), P("row", None)),
        out_specs=P(("row", "depth"), "col"),
        check_vma=False,
    )
```

```python
import functools

import jax
import jax.numpy as jnp
from jax import lax
from jax.experimental import pallas as pl
from jax.experimental.pallas import tpu as pltpu
from jax.sharding import PartitionSpec as P

MESH = pl.DeviceIdType.MESH
NZ, NY, NX = 8, 4, 4
ENV = 128
PTS = 1024
BLK = 256
NT = (((1,), (1,)), ((), ()))
F32, BF16 = jnp.float32, jnp.bfloat16


def nt(a, b):
    return lax.dot_general(a, b, NT, preferred_element_type=F32)


def halves(v):
    hi = v.astype(BF16)
    return hi, (v - hi.astype(F32)).astype(BF16)


def body(scale, env_ref, sp_ref, out_ref, sf, shi, slo, eg, ec, kf, khi, klo, kx,
         jhi, jlo, tt, zn, zf, fr, ft, fs, yt, acc, loc, ssem, rsem):
    d, r, x = lax.axis_index("depth"), lax.axis_index("row"), lax.axis_index("col")
    z, y, core, yl = d // NY, d % NY, r % 2, r // 2
    sib = r + 1 - 2 * core
    mate = (r + 2) * (1 - yl) + (3 - r) * yl
    user = (3 - r) * (1 - yl) + (r - 2) * yl
    right, left = (x + 1) % NX, (x + NX - 1) % NX

    def at_x(c):
        return (d, r, c)

    def at_row(q):
        return (d, q, x)

    def at_z(k):
        return (((z + k) % NZ) * NY + y, r, x)

    def at_y(k):
        return (z * NY + (y + k) % NY, r, x)

    count = [0, 0]
    sends = []

    def new_recv():
        count[1] += 1
        return count[1] - 1

    def send(src, dst, to, dev, when=None):
        c = pltpu.make_async_remote_copy(
            src_ref=src, dst_ref=dst, send_sem=ssem.at[count[0]],
            recv_sem=rsem.at[to], device_id=dev, device_id_type=MESH)
        count[0] += 1
        sends.append((when, c))
        only(when, c.start)

    def only(when, act):
        if when is None:
            act()
        else:
            pl.when(when)(act)

    def arrived(ref, sem):
        pltpu.make_async_copy(ref, ref, rsem.at[sem]).wait()

    load_e = pltpu.make_async_copy(env_ref, eg.at[0], loc.at[0])
    load_e.start()
    loads = []
    for i in range(4):
        rows = pl.ds(i * 256, 256)
        c = pltpu.make_async_copy(sp_ref.at[rows], sf.at[rows], loc.at[1 + i])
        c.start()
        loads.append(c)

    bar = pltpu.get_barrier_semaphore()

    def greet(dev):
        pl.semaphore_signal(bar, inc=1, device_id=dev, device_id_type=MESH)

    greet(at_x(left))
    greet(at_x(right))
    greet(at_row(sib))
    greet(at_row(mate))
    greet(at_z(1))
    greet(at_z(NZ - 1))
    for k in range(1, NY):
        greet(at_y(k))
    pl.semaphore_wait(bar, 9)

    def piece(slot, half, p):
        return eg.at[slot, pl.ds(pl.multiple_of(half * 64 + p * 32, 32), 32)]

    def own(p):
        return env_ref.at[pl.ds(pl.multiple_of(core * 64 + p * 32, 32), 32)]

    ring = {(s, p): new_recv() for s in (1, 2, 3) for p in (0, 1)}
    pair = {(s, p): new_recv() for s in (1, 2, 3) for p in (0, 1)}
    send(own(0), piece(1, core, 0), ring[1, 0], at_x(right))
    send(own(1), piece(2, core, 1), ring[2, 1], at_x(left))
    send(own(1), piece(1, core, 1), ring[1, 1], at_x(right))
    send(own(0), piece(2, core, 0), ring[2, 0], at_x(left))

    def to_sib(s, p):
        send(piece(s, core, p), piece(s, core, p), pair[s, p], at_row(sib))

    for i in range(4):
        loads[i].wait()

        @pl.loop(0, 4)
        def _(j):
            rows = pl.ds(pl.multiple_of(i * 256 + j * 64, 64), 64)
            hi, lo = halves(sf[rows])
            shi[rows] = hi
            slo[rows] = lo

    load_e.wait()

    mine = pl.ds(pl.multiple_of(x * BLK, BLK), BLK)
    krecv = {(w, s): new_recv() for w in (0, 1) for s in range(4)}

    def shard(s):
        hi, lo = halves(eg[s])
        ec[0:ENV] = hi
        ec[ENV:] = lo
        cols = slice(s * ENV, (s + 1) * ENV)

        @pl.loop(0, 4)
        def _(i):
            rows = pl.ds(pl.multiple_of(i * 256, 256), 256)
            both = nt(shi[rows], ec[...])
            low = nt(slo[rows], ec[0:ENV])
            dots = both[:, :ENV] + (both[:, ENV:] + low)
            sq = dots * dots
            k = sq * sq
            kf[s, rows] = k
            a, b = halves(k)
            khi[rows, cols] = a
            klo[rows, cols] = b

        send(kf.at[s, mine], kx.at[0, s], krecv[0, s], at_row(sib), core == 1)
        send(kf.at[s, mine], kx.at[1, s], krecv[1, s], at_row(user))

    shard(0)
    arrived(piece(1, core, 0), ring[1, 0])
    send(piece(1, core, 0), piece(3, core, 0), ring[3, 0], at_x(right))
    to_sib(1, 0)
    arrived(piece(2, core, 1), ring[2, 1])
    send(piece(2, core, 1), piece(3, core, 1), ring[3, 1], at_x(left))
    to_sib(2, 1)
    arrived(piece(1, core, 1), ring[1, 1])
    to_sib(1, 1)
    arrived(piece(2, core, 0), ring[2, 0])
    to_sib(2, 0)
    arrived(piece(1, 1 - core, 0), pair[1, 0])
    arrived(piece(1, 1 - core, 1), pair[1, 1])
    shard(1)
    arrived(piece(3, core, 0), ring[3, 0])
    to_sib(3, 0)
    arrived(piece(3, core, 1), ring[3, 1])
    to_sib(3, 1)
    arrived(piece(2, 1 - core, 1), pair[2, 1])
    arrived(piece(2, 1 - core, 0), pair[2, 0])
    shard(2)
    arrived(piece(3, 1 - core, 0), pair[3, 0])
    arrived(piece(3, 1 - core, 1), pair[3, 1])
    shard(3)

    even = core == 0
    near = {(b, t): new_recv() for b in range(6) for t in range(4)}
    far = {(b, t): new_recv() for b in range(6) for t in range(3)}

    def gram(p, rhi, rlo):
        @pl.loop(0, 4)
        def _(i):
            rows = pl.ds(pl.multiple_of(i * 256, 256), 256)
            a = khi[rows]
            g = nt(a, rhi) + (nt(a, rlo) + nt(klo[rows], rhi))
            for h in range(2):
                for q in range(2):
                    tt[2 * p + h, 2 * i + q] = g[q * 128:(q + 1) * 128, h * 128:(h + 1) * 128]

    def received(w):
        for s in range(4):
            arrived(kx.at[w, s], krecv[w, s])
            hi, lo = halves(kx[w, s])
            jhi[w, :, s * ENV:(s + 1) * ENV] = hi
            jlo[w, :, s * ENV:(s + 1) * ENV] = lo
        gram(1 + w, jhi[w], jlo[w])

    def gap(b, c):
        return (c + 2 * NZ - 2 * x - b % 2) % NZ

    def held(b, c):
        return (gap(b, c) <= 4, even, None)[b // 2]

    def turned(b):
        return ((gap(b, z) >= 1) & (gap(b, z) <= 3), even, None)[b // 2]

    def zsend(b, t):
        m = 1 - 2 * (b % 2)
        c = (z + NZ + m * (4 - t)) % NZ
        send(tt.at[b, c], zn.at[b, t], near[b, t], at_z(m % NZ), held(b, c))
        if t < 3:
            c = (z + NZ - m * (3 - t)) % NZ
            send(tt.at[b, c], zf.at[b, t], far[b, t], at_z(-m % NZ), held(b, c))

    def zstep(b, t):
        m = 1 - 2 * (b % 2)

        def take(c, slot, sem):
            def act():
                arrived(slot, sem)
                tt[b, c] = tt[b, c] + slot[...]
            only(held(b, c), act)

        take((z + NZ + m * (3 - t)) % NZ, zn.at[b, t], near[b, t])
        if t < 3:
            take((z + NZ - m * (2 - t)) % NZ, zf.at[b, t], far[b, t])
            zsend(b, t + 1)

    own_y = pl.ds(pl.multiple_of(y * 32, 32), 32)
    ytail = {(b, k): new_recv() for b in range(6) for k in range(1, NY)}
    last = [new_recv() for _ in range(8)]
    dest = (r, sib, mate)

    def finish(b):
        p, h, when = b // 2, b % 2, held(b, z)
        g = 2 * x + h
        here, away = x == dest[p], x != dest[p]
        if when is not None:
            here, away = here & when, away & when

        def act():
            fr[b] = tt[b, z] * scale

        only(when, act)
        for k in range(NY):
            yy = (y + k) % NY
            rows = pl.ds(pl.multiple_of(yy * 32, 32), 32)
            if k == 0:
                @pl.when(here)
                def _():
                    acc[g, y] = fr[b, rows]
            send(fr.at[b, rows], acc.at[g, y], last[0] + g, (z * NY + yy, r, dest[p]), when if k else away)

        def flip():
            ft[b] = fr[b].T

        only(turned(b), flip)
        for k in range(1, NY):
            rows = pl.ds(pl.multiple_of(((y + k) % NY) * 32, 32), 32)
            send(ft.at[b, rows], yt.at[b, k - 1], ytail[b, k], at_y(k), turned(b))

    def settle(b):
        p, g = b // 2, 2 * x + b % 2

        def act():
            for k in range(1, NY):
                arrived(yt.at[b, k - 1], ytail[b, k])
            fs[b] = (ft[b, own_y] + yt[b, 0]) + (yt[b, 1] + yt[b, 2])

        only(turned(b), act)
        send(fs.at[b], acc.at[z, 0], last[0] + z, (g * NY + y, dest[p], r), turned(b))

    gram(0, khi[mine], klo[mine])
    zsend(0, 0)
    zsend(1, 0)
    only(even, lambda: received(0))
    zsend(2, 0)
    zsend(3, 0)
    zstep(0, 0)
    zstep(1, 0)
    received(1)
    zsend(4, 0)
    zsend(5, 0)
    for p, t in ((1, 0), (0, 1), (1, 1), (2, 0), (0, 2), (1, 2), (2, 1), (0, 3), (1, 3), (2, 2), (2, 3)):
        for b in (2 * p, 2 * p + 1):
            zstep(b, t)
            if t == 3:
                finish(b)
        if (p, t) == (2, 2):
            for b in range(4):
                settle(b)
    settle(4)
    settle(5)

    for g in range(8):
        mirrored = (x == user) | ((x == sib) & (core == 1)) | ((x == r) & ((z + NZ - g) % NZ >= 5))
        cols = slice(g * 128, (g + 1) * 128)

        @pl.when(mirrored)
        def _():
            arrived(acc.at[g, 0], last[g])
            out_ref[:, cols] = acc[g, 0]

        @pl.when(jnp.logical_not(mirrored))
        def _():
            @pl.when(x != g // 2)
            def _():
                arrived(acc.at[g], last[g])

            @pl.when(x == g // 2)
            def _():
                arrived(acc.at[g, 0:3], last[g])

            out_ref[:, cols] = (acc[g, 0] + acc[g, 1]) + (acc[g, 2] + acc[g, 3])

    for when, c in sends:
        only(when, c.wait_send)


def per_device(total, env_desc, sparse_desc):
    vm = pltpu.VMEM
    width = env_desc.shape[1]
    return pl.pallas_call(
        functools.partial(body, 1.0 / total),
        out_shape=jax.ShapeDtypeStruct((32, PTS), F32),
        in_specs=[pl.BlockSpec(memory_space=pl.ANY)] * 2,
        out_specs=pl.BlockSpec(memory_space=pltpu.VMEM),
        scratch_shapes=[
            vm((PTS, width), F32), vm((PTS, width), BF16), vm((PTS, width), BF16),
            vm((4, ENV, width), F32), vm((2 * ENV, width), BF16),
            vm((4, PTS, ENV), F32), vm((PTS, 4 * ENV), BF16), vm((PTS, 4 * ENV), BF16),
            vm((2, 4, BLK, ENV), F32),
            vm((2, BLK, 4 * ENV), BF16), vm((2, BLK, 4 * ENV), BF16),
            vm((6, NZ, 128, 128), F32),
            vm((6, 4, 128, 128), F32), vm((6, 3, 128, 128), F32),
            vm((6, 128, 128), F32), vm((6, 128, 128), F32), vm((6, 32, 128), F32),
            vm((6, NY - 1, 32, 128), F32), vm((8, NY, 32, 128), F32),
            pltpu.SemaphoreType.DMA((5,)),
            pltpu.SemaphoreType.DMA((120,)),
            pltpu.SemaphoreType.DMA((88,)),
        ],
        compiler_params=pltpu.CompilerParams(
            collective_id=0, has_side_effects=True, vmem_limit_bytes=60 * 2 ** 20),
        cost_estimate=pl.CostEstimate(
            flops=6 * 4 * ENV * PTS * (width + 768), bytes_accessed=5 * 2 ** 20, transcendentals=0),
    )(env_desc, sparse_desc)


def solution(mesh):
    total = ENV * mesh.shape["depth"] * mesh.shape["col"]
    return jax.shard_map(
        functools.partial(per_device, total),
        mesh=mesh,
        in_specs=(P(("depth", "col"), None), P("row", None)),
        out_specs=P(("row", "depth"), "col"),
        check_vma=False,
    )
```

```python
import functools

import jax
import jax.numpy as jnp
from jax import lax
from jax.experimental import pallas as pl
from jax.experimental.pallas import tpu as pltpu
from jax.sharding import PartitionSpec as P

MESH = pl.DeviceIdType.MESH
NZ, NY, NX = 8, 4, 4
ENV = 128
PTS = 1024
BLK = 256
NT = (((1,), (1,)), ((), ()))
F32, BF16 = jnp.float32, jnp.bfloat16


def nt(a, b):
    return lax.dot_general(a, b, NT, preferred_element_type=F32)


def halves(v):
    hi = v.astype(BF16)
    return hi, (v - hi.astype(F32)).astype(BF16)


def body(scale, env_ref, sp_ref, out_ref, sf, shi, slo, eg, ec, kf, khi, klo, kx,
         jhi, jlo, tt, zn, zf, yn, yf, zt, fr, ft, fs, yt, acc, tp, tr, loc, ssem, rsem):
    d, r, x = lax.axis_index("depth"), lax.axis_index("row"), lax.axis_index("col")
    z, y, core, yl = d // NY, d % NY, r % 2, r // 2
    sib = r + 1 - 2 * core
    mate = (r + 2) * (1 - yl) + (3 - r) * yl
    user = (3 - r) * (1 - yl) + (r - 2) * yl
    right, left = (x + 1) % NX, (x + NX - 1) % NX

    def at_x(c):
        return (d, r, c)

    def at_row(q):
        return (d, q, x)

    def at_z(k):
        return (((z + k) % NZ) * NY + y, r, x)

    def at_y(k):
        return (z * NY + (y + k) % NY, r, x)

    count = [0, 0]
    sends = []

    def new_recv():
        count[1] += 1
        return count[1] - 1

    def send(src, dst, to, dev, when=None):
        c = pltpu.make_async_remote_copy(
            src_ref=src, dst_ref=dst, send_sem=ssem.at[count[0]],
            recv_sem=rsem.at[to], device_id=dev, device_id_type=MESH)
        count[0] += 1
        sends.append((when, c))
        only(when, c.start)

    def only(when, act):
        if when is None:
            act()
        else:
            pl.when(when)(act)

    def arrived(ref, sem):
        pltpu.make_async_copy(ref, ref, rsem.at[sem]).wait()

    load_e = pltpu.make_async_copy(env_ref, eg.at[0], loc.at[0])
    load_e.start()
    loads = []
    for i in range(4):
        rows = pl.ds(i * 256, 256)
        c = pltpu.make_async_copy(sp_ref.at[rows], sf.at[rows], loc.at[1 + i])
        c.start()
        loads.append(c)

    bar = pltpu.get_barrier_semaphore()

    def greet(dev):
        pl.semaphore_signal(bar, inc=1, device_id=dev, device_id_type=MESH)

    greet(at_x(left))
    greet(at_x(right))
    greet(at_row(sib))
    greet(at_row(mate))
    for k in range(1, NZ):
        greet(at_z(k))
    for k in range(1, NY):
        greet(at_y(k))
    pl.semaphore_wait(bar, 14)

    def piece(side, half, p):
        if side == 3:
            return eg.at[3, pl.ds(pl.multiple_of(half * 64 + p * 32, 32), 32)]
        slot = 1 if side == 1 + p else 2
        return eg.at[slot, pl.ds(pl.multiple_of(half * 32 + (side - 1) * 64, 32), 32)]

    def own(p):
        return env_ref.at[pl.ds(pl.multiple_of(core * 64 + p * 32, 32), 32)]

    ring = {(s, p): new_recv() for s in (1, 2, 3) for p in (0, 1)}
    pair = {(s, p): new_recv() for s in (1, 2, 3) for p in (0, 1)}
    send(own(0), piece(1, core, 0), ring[1, 0], at_x(right))
    send(own(1), piece(2, core, 1), ring[2, 1], at_x(left))
    send(own(1), piece(1, core, 1), ring[1, 1], at_x(right))
    send(own(0), piece(2, core, 0), ring[2, 0], at_x(left))

    def to_sib(s, p):
        send(piece(s, core, p), piece(s, core, p), pair[s, p], at_row(sib))

    for i in range(4):
        loads[i].wait()

        @pl.loop(0, 4)
        def _(j):
            rows = pl.ds(pl.multiple_of(i * 256 + j * 64, 64), 64)
            hi, lo = halves(sf[rows])
            shi[rows] = hi
            slo[rows] = lo

    load_e.wait()

    mine = pl.ds(pl.multiple_of(x * BLK, BLK), BLK)
    krecv = {(w, s): new_recv() for w in (0, 1) for s in range(4)}

    def shard(s):
        hi, lo = halves(eg[s])
        ec[0:ENV] = hi
        ec[ENV:] = lo
        cols = slice(s * ENV, (s + 1) * ENV)

        @pl.loop(0, 4)
        def _(i):
            rows = pl.ds(pl.multiple_of(i * 256, 256), 256)
            both = nt(shi[rows], ec[...])
            low = nt(slo[rows], ec[0:ENV])
            dots = both[:, :ENV] + (both[:, ENV:] + low)
            sq = dots * dots
            k = sq * sq
            kf[s, rows] = k
            a, b = halves(k)
            khi[rows, cols] = a
            klo[rows, cols] = b

        send(kf.at[s, mine], kx.at[0, s], krecv[0, s], at_row(sib), core == 1)
        send(kf.at[s, mine], kx.at[1, s], krecv[1, s], at_row(user))

    shard(0)
    arrived(piece(1, core, 0), ring[1, 0])
    send(piece(1, core, 0), piece(3, core, 0), ring[3, 0], at_x(right))
    to_sib(1, 0)
    arrived(piece(2, core, 1), ring[2, 1])
    send(piece(2, core, 1), piece(3, core, 1), ring[3, 1], at_x(left))
    to_sib(2, 1)
    arrived(piece(1, 1 - core, 0), pair[1, 0])
    arrived(piece(2, 1 - core, 1), pair[2, 1])
    shard(1)
    for side, p in ((1, 1), (2, 0)):
        arrived(piece(side, core, p), ring[side, p])
        to_sib(side, p)
    for side, p in ((1, 1), (2, 0)):
        arrived(piece(side, 1 - core, p), pair[side, p])
    shard(2)
    for p in (0, 1):
        arrived(piece(3, core, p), ring[3, p])
        to_sib(3, p)
    for p in (0, 1):
        arrived(piece(3, 1 - core, p), pair[3, p])
    shard(3)

    even = core == 0
    zblocks, yblocks = (0, 1, 4, 5), (2, 3)
    near = {(b, t): new_recv() for b in zblocks for t in range(4)}
    far = {(b, t): new_recv() for b in zblocks for t in range(3)}
    ynear = {(b, t): new_recv() for b in yblocks for t in range(2)}
    yfar = {b: new_recv() for b in yblocks}
    ztail = {(b, k): new_recv() for b in yblocks for k in range(1, NZ)}

    def gram(p, rhi, rlo):
        @pl.loop(0, 4)
        def _(i):
            rows = pl.ds(pl.multiple_of(i * 256, 256), 256)
            a = khi[rows]
            g = nt(a, rhi) + (nt(a, rlo) + nt(klo[rows], rhi))
            for h in range(2):
                for q in range(2):
                    tt[2 * p + h, 2 * i + q] = g[q * 128:(q + 1) * 128, h * 128:(h + 1) * 128]

    def received(w):
        for s in range(4):
            arrived(kx.at[w, s], krecv[w, s])
            hi, lo = halves(kx[w, s])
            jhi[w, :, s * ENV:(s + 1) * ENV] = hi
            jlo[w, :, s * ENV:(s + 1) * ENV] = lo
        gram(1 + w, jhi[w], jlo[w])

    def gap(b, c):
        return (c + 2 * NZ - 2 * x - b % 2) % NZ

    def held(b, c):
        return (gap(b, c) <= 4, even, None)[b // 2]

    def turned(b):
        return ((gap(b, z) >= 1) & (gap(b, z) <= 3), even, None)[b // 2]

    def zsend(b, t):
        m = 1 - 2 * (b % 2)
        c = (z + NZ + m * (4 - t)) % NZ
        send(tt.at[b, c], zn.at[zblocks.index(b), t], near[b, t], at_z(m % NZ), held(b, c))
        if t < 3:
            c = (z + NZ - m * (3 - t)) % NZ
            send(tt.at[b, c], zf.at[zblocks.index(b), t], far[b, t], at_z(-m % NZ), held(b, c))

    def zstep(b, t):
        m = 1 - 2 * (b % 2)

        def take(c, slot, sem):
            def act():
                arrived(slot, sem)
                tt[b, c] = tt[b, c] + slot[...]
            only(held(b, c), act)

        take((z + NZ + m * (3 - t)) % NZ, zn.at[zblocks.index(b), t], near[b, t])
        if t < 3:
            take((z + NZ - m * (2 - t)) % NZ, zf.at[zblocks.index(b), t], far[b, t])
            zsend(b, t + 1)

    own_y = pl.ds(pl.multiple_of(y * 32, 32), 32)

    def ychunk(k):
        return pl.ds(pl.multiple_of(((y + k) % NY) * 32, 32), 32)

    def ysend(b, t):
        m = 1 - 2 * (b % 2)
        c = ychunk((2 - t) * m % NY)
        send(tt.at[b, :, c], yn.at[b - 2, t], ynear[b, t], at_y(m % NY), even)
        if t == 0:
            send(tt.at[b, :, ychunk(-m % NY)], yf.at[b - 2], yfar[b], at_y(-m % NY), even)

    def ystep(b, t):
        m = 1 - 2 * (b % 2)
        c = ychunk((1 - t) * m % NY)

        def act():
            arrived(yn.at[b - 2, t], ynear[b, t])
            tt[b, :, c] = tt[b, :, c] + yn[b - 2, t]
            if t == 1:
                arrived(yf.at[b - 2], yfar[b])
                tt[b, :, c] = tt[b, :, c] + yf[b - 2]

        only(even, act)
        if t == 0:
            ysend(b, 1)
        else:
            for k in range(1, NZ):
                send(tt.at[b, (z + k) % NZ, own_y], zt.at[b - 2, k - 1], ztail[b, k], at_z(k), even)

    ytail = {(b, k): new_recv() for b in zblocks for k in range(1, NY)}
    last = [new_recv() for _ in range(8)]
    dest = (r, sib, mate)

    def finish(b):
        p, h, when = b // 2, b % 2, held(b, z)
        g = 2 * x + h
        here, away = x == dest[p], x != dest[p]
        if when is not None:
            here, away = here & when, away & when

        def flip():
            ft[b] = (tt[b, z] * scale).T

        only(turned(b), flip)
        for k in range(1, NY):
            rows = pl.ds(pl.multiple_of(((y + k) % NY) * 32, 32), 32)
            send(ft.at[b, rows], yt.at[zblocks.index(b), k - 1], ytail[b, k], at_y(k), turned(b))

        def keep():
            fr[b] = tt[b, z] * scale

        only(when, keep)
        for k in range(NY):
            yy = (y + k) % NY
            rows = pl.ds(pl.multiple_of(yy * 32, 32), 32)
            if k == 0:
                @pl.when(here)
                def _():
                    acc[g, y] = fr[b, rows]
            send(fr.at[b, rows], acc.at[g, y], last[0] + g, (z * NY + yy, r, dest[p]), when if k else away)

    def settle(b):
        p, g = b // 2, 2 * x + b % 2

        def act():
            for k in range(1, NY):
                arrived(yt.at[zblocks.index(b), k - 1], ytail[b, k])
            i = zblocks.index(b)
            fs[b] = (ft[b, own_y] + yt[i, 0]) + (yt[i, 1] + yt[i, 2])

        only(turned(b), act)
        send(fs.at[b], acc.at[z, 0], last[0] + z, (g * NY + y, dest[p], r), turned(b))

    lane = lax.broadcasted_iota(jnp.int32, (8, 128), 1) // 32

    def close(b):
        g = 2 * x + b % 2

        def act():
            v = tt[b, z, own_y]
            for k in range(1, NZ):
                arrived(zt.at[b - 2, k - 1], ztail[b, k])
                v = v + zt[b - 2, k - 1]
            v = v * scale
            fs[b] = v
            turn = jnp.concatenate([v, jnp.zeros((96, 128), F32)], axis=0).T
            for q in range(4):
                w = jnp.zeros((8, 128), F32)
                for i in range(4):
                    rows = turn[q * 32 + i * 8:q * 32 + i * 8 + 8]
                    w = jnp.where(lane == i, pltpu.roll(rows, i * 32, 1) if i else rows, w)
                tp[b - 2, q] = w

        only(even, act)
        for q in range(4):
            send(tp.at[b - 2, q], tr.at[d], last[0] + z, (4 * g + q, sib, r), even)

        @pl.when(even & (x == sib))
        def _():
            acc[g, 0] = fs[b]

        send(fs.at[b], acc.at[g, 0], last[0] + g, at_x(sib), even & (x != sib))

    gram(0, khi[mine], klo[mine])
    zsend(0, 0)
    zsend(1, 0)
    only(even, lambda: received(0))
    ysend(2, 0)
    ysend(3, 0)
    zstep(0, 0)
    zstep(1, 0)
    received(1)
    zsend(4, 0)
    zsend(5, 0)
    for act, blocks, t in ((zstep, (0, 1), 1), (zstep, (4, 5), 0), (ystep, (2, 3), 0), (zstep, (0, 1), 2),
                           (zstep, (4, 5), 1), (ystep, (2, 3), 1), (zstep, (0, 1), 3), (zstep, (4, 5), 2)):
        for b in blocks:
            act(b, t)
            if t == 3:
                finish(b)
    for b in (0, 1):
        settle(b)
    for b in (4, 5):
        zstep(b, 3)
        finish(b)
    for b in (2, 3):
        close(b)
    for b in (4, 5):
        settle(b)

    for g in range(8):
        mirrored = (x == user) | ((x == r) & ((z + NZ - g) % NZ >= 5))
        plain = ((x == r) & ((z + NZ - g) % NZ <= 4)) | (x == mate)
        cols = slice(g * 128, (g + 1) * 128)

        @pl.when(mirrored)
        def _():
            arrived(acc.at[g, 0], last[g])
            out_ref[:, cols] = acc[g, 0]

        @pl.when(plain)
        def _():
            @pl.when(x != g // 2)
            def _():
                arrived(acc.at[g], last[g])

            @pl.when(x == g // 2)
            def _():
                arrived(acc.at[g, 0:3], last[g])

            out_ref[:, cols] = (acc[g, 0] + acc[g, 1]) + (acc[g, 2] + acc[g, 3])

        @pl.when((x == sib) & even)
        def _():
            @pl.when(x != g // 2)
            def _():
                arrived(acc.at[g, 0], last[g])

            out_ref[:, cols] = acc[g, 0]

        @pl.when((x == sib) & jnp.logical_not(even))
        def _():
            arrived(tr.at[4 * g:4 * g + 4], last[g])
            for q in range(4):
                v = jnp.zeros((8, 128), F32)
                for i in range(NY):
                    rows = tr[g * NY + i]
                    turn = ((i - q) * 32) % 128
                    v = jnp.where(lane == i, pltpu.roll(rows, turn, 1) if turn else rows, v)
                out_ref[q * 8:q * 8 + 8, cols] = v

    for when, c in sends:
        only(when, c.wait_send)


def per_device(total, env_desc, sparse_desc):
    vm = pltpu.VMEM
    width = env_desc.shape[1]
    return pl.pallas_call(
        functools.partial(body, 1.0 / total),
        out_shape=jax.ShapeDtypeStruct((32, PTS), F32),
        in_specs=[pl.BlockSpec(memory_space=pl.ANY)] * 2,
        out_specs=pl.BlockSpec(memory_space=pltpu.VMEM),
        scratch_shapes=[
            vm((PTS, width), F32), vm((PTS, width), BF16), vm((PTS, width), BF16),
            vm((4, ENV, width), F32), vm((2 * ENV, width), BF16),
            vm((4, PTS, ENV), F32), vm((PTS, 4 * ENV), BF16), vm((PTS, 4 * ENV), BF16),
            vm((2, 4, BLK, ENV), F32),
            vm((2, BLK, 4 * ENV), BF16), vm((2, BLK, 4 * ENV), BF16),
            vm((6, NZ, 128, 128), F32),
            vm((4, 4, 128, 128), F32), vm((4, 3, 128, 128), F32),
            vm((2, 2, NZ, 32, 128), F32), vm((2, NZ, 32, 128), F32), vm((2, NZ - 1, 32, 128), F32),
            vm((6, 128, 128), F32), vm((6, 128, 128), F32), vm((6, 32, 128), F32),
            vm((4, NY - 1, 32, 128), F32), vm((8, NY, 32, 128), F32),
            vm((2, 4, 8, 128), F32), vm((NZ * NY, 8, 128), F32),
            pltpu.SemaphoreType.DMA((5,)),
            pltpu.SemaphoreType.DMA((120,)),
            pltpu.SemaphoreType.DMA((88,)),
        ],
        compiler_params=pltpu.CompilerParams(
            collective_id=0, has_side_effects=True, vmem_limit_bytes=60 * 2 ** 20),
        cost_estimate=pl.CostEstimate(
            flops=6 * 4 * ENV * PTS * (width + 768), bytes_accessed=5 * 2 ** 20, transcendentals=0),
    )(env_desc, sparse_desc)


def solution(mesh):
    total = ENV * mesh.shape["depth"] * mesh.shape["col"]
    return jax.shard_map(
        functools.partial(per_device, total),
        mesh=mesh,
        in_specs=(P(("depth", "col"), None), P("row", None)),
        out_specs=P(("row", "depth"), "col"),
        check_vma=False,
    )
```

```python
import functools

import jax
import jax.numpy as jnp
from jax import lax
from jax.experimental import pallas as pl
from jax.experimental.pallas import tpu as pltpu
from jax.sharding import PartitionSpec as P

MESH = pl.DeviceIdType.MESH
NZ, NY, NX = 8, 4, 4
ENV = 128
PTS = 1024
BLK = 256
NT = (((1,), (1,)), ((), ()))
F32, BF16 = jnp.float32, jnp.bfloat16


def nt(a, b):
    return lax.dot_general(a, b, NT, preferred_element_type=F32)


def halves(v):
    hi = v.astype(BF16)
    return hi, (v - hi.astype(F32)).astype(BF16)


def body(scale, env_ref, sp_ref, out_ref, sf, shi, slo, eg, ec, kf, khi, klo, kx,
         jhi, jlo, tt, zn, zf, yn, yf, zt, fr, ft, fs, yt, acc, tp, tr, loc, ssem, rsem):
    d, r, x = lax.axis_index("depth"), lax.axis_index("row"), lax.axis_index("col")
    z, y, core, yl = d // NY, d % NY, r % 2, r // 2
    sib = r + 1 - 2 * core
    mate = (r + 2) * (1 - yl) + (3 - r) * yl
    user = (3 - r) * (1 - yl) + (r - 2) * yl
    right, left = (x + 1) % NX, (x + NX - 1) % NX

    def at_x(c):
        return (d, r, c)

    def at_row(q):
        return (d, q, x)

    def at_z(k):
        return (((z + k) % NZ) * NY + y, r, x)

    def at_y(k):
        return (z * NY + (y + k) % NY, r, x)

    count = [0, 0]
    sends = []

    def new_recv():
        count[1] += 1
        return count[1] - 1

    groups = {}

    def send(src, dst, to, dev, when=None, group=None):
        sem = count[0] if group is None else groups.get(group[:2], count[0])
        c = pltpu.make_async_remote_copy(
            src_ref=src, dst_ref=dst, send_sem=ssem.at[sem],
            recv_sem=rsem.at[to], device_id=dev, device_id_type=MESH)
        if sem == count[0]:
            count[0] += 1
            if group is None:
                sends.append((when, c.wait_send))
            else:
                groups[group[:2]] = sem
                sends.append((when, pltpu.make_async_copy(group[2], group[2], ssem.at[sem]).wait))
        only(when, c.start)

    def only(when, act):
        if when is None:
            act()
        else:
            pl.when(when)(act)

    def arrived(ref, sem):
        pltpu.make_async_copy(ref, ref, rsem.at[sem]).wait()

    load_e = pltpu.make_async_copy(env_ref, eg.at[0], loc.at[0])
    load_e.start()
    loads = []
    for i in range(4):
        rows = pl.ds(i * 256, 256)
        c = pltpu.make_async_copy(sp_ref.at[rows], sf.at[rows], loc.at[1 + i])
        c.start()
        loads.append(c)

    bar = pltpu.get_barrier_semaphore()

    def greet(dev):
        pl.semaphore_signal(bar, inc=1, device_id=dev, device_id_type=MESH)

    greet(at_x(left))
    greet(at_x(right))
    greet(at_row(sib))
    greet(at_row(mate))
    for k in range(1, NZ):
        greet(at_z(k))
    for k in range(1, NY):
        greet(at_y(k))
    pl.semaphore_wait(bar, 14)

    def piece(side, half, p):
        if side == 3:
            return eg.at[3, pl.ds(pl.multiple_of(half * 64 + p * 32, 32), 32)]
        slot = 1 if side == 1 + p else 2
        return eg.at[slot, pl.ds(pl.multiple_of(half * 32 + (side - 1) * 64, 32), 32)]

    def own(p):
        return env_ref.at[pl.ds(pl.multiple_of(core * 64 + p * 32, 32), 32)]

    ring = {(s, p): new_recv() for s in (1, 2, 3) for p in (0, 1)}
    pair = {(s, p): new_recv() for s in (1, 2, 3) for p in (0, 1)}
    send(own(0), piece(1, core, 0), ring[1, 0], at_x(right))
    send(own(1), piece(2, core, 1), ring[2, 1], at_x(left))
    send(own(1), piece(1, core, 1), ring[1, 1], at_x(right))
    send(own(0), piece(2, core, 0), ring[2, 0], at_x(left))

    def to_sib(s, p):
        send(piece(s, core, p), piece(s, core, p), pair[s, p], at_row(sib))

    for i in range(4):
        loads[i].wait()

        @pl.loop(0, 4)
        def _(j):
            rows = pl.ds(pl.multiple_of(i * 256 + j * 64, 64), 64)
            hi, lo = halves(sf[rows])
            shi[rows] = hi
            slo[rows] = lo

    load_e.wait()

    mine = pl.ds(pl.multiple_of(x * BLK, BLK), BLK)
    krecv = {(w, s): new_recv() for w in (0, 1) for s in range(4)}

    def shard(s):
        hi, lo = halves(eg[s])
        ec[0:ENV] = hi
        ec[ENV:] = lo
        cols = slice(s * ENV, (s + 1) * ENV)

        def some(i, c):
            rows = pl.ds(pl.multiple_of(((x + i) % 4) * 256, 256), 256)
            both = nt(shi[rows], ec[...])
            low = nt(slo[rows], ec[0:ENV])
            dots = both[:, :ENV] + (both[:, ENV:] + low)
            sq = dots * dots
            k = sq * sq
            kf[s, rows] = k
            a, b = halves(k)
            khi[rows, cols] = a
            klo[rows, cols] = b
            return c

        some(0, 0)
        send(kf.at[s, mine], kx.at[1, s], krecv[1, s], at_row(user))
        send(kf.at[s, mine], kx.at[0, s], krecv[0, s], at_row(sib), core == 1)
        lax.fori_loop(1, 4, some, 0)

    shard(0)
    arrived(piece(1, core, 0), ring[1, 0])
    send(piece(1, core, 0), piece(3, core, 0), ring[3, 0], at_x(right))
    to_sib(1, 0)
    arrived(piece(2, core, 1), ring[2, 1])
    send(piece(2, core, 1), piece(3, core, 1), ring[3, 1], at_x(left))
    to_sib(2, 1)
    arrived(piece(1, 1 - core, 0), pair[1, 0])
    arrived(piece(2, 1 - core, 1), pair[2, 1])
    shard(1)
    for side, p in ((1, 1), (2, 0)):
        arrived(piece(side, core, p), ring[side, p])
        to_sib(side, p)
    for side, p in ((1, 1), (2, 0)):
        arrived(piece(side, 1 - core, p), pair[side, p])
    shard(2)
    for p in (0, 1):
        arrived(piece(3, core, p), ring[3, p])
        to_sib(3, p)
    for p in (0, 1):
        arrived(piece(3, 1 - core, p), pair[3, p])
    shard(3)

    even = core == 0
    zblocks, yblocks = (0, 1, 4, 5), (2, 3)
    near = {(b, t, u): new_recv() for b in zblocks for t in range(4) for u in range(2)}
    far = {(b, t, u): new_recv() for b in zblocks for t in range(3) for u in range(2)}
    ynear = {(b, t): new_recv() for b in yblocks for t in range(2)}
    yfar = {b: new_recv() for b in yblocks}
    ztail = {b: new_recv() for b in yblocks}

    def gram(p, rhi, rlo):
        @pl.loop(0, 4)
        def _(i):
            rows = pl.ds(pl.multiple_of(i * 256, 256), 256)
            a = khi[rows]
            g = nt(a, rhi) + (nt(a, rlo) + nt(klo[rows], rhi))
            for h in range(2):
                for q in range(2):
                    tt[2 * p + h, 2 * i + q] = g[q * 128:(q + 1) * 128, h * 128:(h + 1) * 128]

    def received(w):
        for s in range(4):
            arrived(kx.at[w, s], krecv[w, s])
            hi, lo = halves(kx[w, s])
            jhi[w, :, s * ENV:(s + 1) * ENV] = hi
            jlo[w, :, s * ENV:(s + 1) * ENV] = lo
        gram(1 + w, jhi[w], jlo[w])

    def gap(b, c):
        return (c + 2 * NZ - 2 * x - b % 2) % NZ

    def held(b, c):
        return (gap(b, c) <= 4, even, None)[b // 2]

    def turned(b):
        return ((gap(b, z) >= 1) & (gap(b, z) <= 3), even, None)[b // 2]

    def half(u):
        return pl.ds(u * 64, 64)

    def znear(b, t, u):
        m = 1 - 2 * (b % 2)
        c = (z + NZ + m * (4 - t)) % NZ
        send(tt.at[b, c, half(u)], zn.at[zblocks.index(b), t, half(u)], near[b, t, u], at_z(m % NZ), held(b, c),
             (b, t, zn.at[zblocks.index(b), t]) if b < 2 else (b, 4, zn.at[zblocks.index(b)]))

    def zfar(b, t, u):
        m = 1 - 2 * (b % 2)
        c = (z + NZ - m * (3 - t)) % NZ
        send(tt.at[b, c, half(u)], zf.at[zblocks.index(b), t, half(u)], far[b, t, u], at_z(-m % NZ), held(b, c),
             (b, 8 + t, zf.at[zblocks.index(b), t]) if b < 2 else (b, 12, zf.at[zblocks.index(b)]))

    def zsend(blocks):
        for f in (znear, zfar):
            for u in range(2):
                for b in blocks:
                    f(b, 0, u)

    def zstep(blocks, t):
        def take(b, c, u, slot, sem):
            def act():
                arrived(slot, sem)
                tt[b, c, half(u)] = tt[b, c, half(u)] + slot[...]
            only(held(b, c), act)

        for u in range(2):
            for b in blocks:
                m = 1 - 2 * (b % 2)
                take(b, (z + NZ + m * (3 - t)) % NZ, u, zn.at[zblocks.index(b), t, half(u)], near[b, t, u])
                if t < 3:
                    znear(b, t + 1, u)
                elif u == 1:
                    finish(b)
        if t < 3:
            for u in range(2):
                for b in blocks:
                    m = 1 - 2 * (b % 2)
                    take(b, (z + NZ - m * (2 - t)) % NZ, u, zf.at[zblocks.index(b), t, half(u)], far[b, t, u])
                    if t < 2:
                        zfar(b, t + 1, u)

    own_y = pl.ds(pl.multiple_of(y * 32, 32), 32)

    def ychunk(k):
        return pl.ds(pl.multiple_of(((y + k) % NY) * 32, 32), 32)

    def ynext(b, t):
        m = 1 - 2 * (b % 2)
        send(tt.at[b, :, ychunk((2 - t) * m % NY)], yn.at[b - 2, t], ynear[b, t], at_y(m % NY), even)

    def ysend(blocks):
        for b in blocks:
            ynext(b, 0)
        for b in blocks:
            m = 1 - 2 * (b % 2)
            send(tt.at[b, :, ychunk(-m % NY)], yf.at[b - 2], yfar[b], at_y(-m % NY), even)

    def ystep(blocks, t):
        for b in blocks:
            m = 1 - 2 * (b % 2)
            c = ychunk((1 - t) * m % NY)

            def act():
                arrived(yn.at[b - 2, t], ynear[b, t])
                if t == 0:
                    tt[b, :, c] = tt[b, :, c] + yn[b - 2, t]
                else:
                    arrived(yf.at[b - 2], yfar[b])
                    tt[b, :, c] = tt[b, :, c] + yn[b - 2, t] + yf[b - 2]

            only(even, act)
            if t == 0:
                ynext(b, 1)
            else:
                for k in range(1, NZ):
                    send(tt.at[b, (z + k) % NZ, own_y], zt.at[b - 2, k - 1], ztail[b], at_z(k), even, (b, 20, zt.at[b - 2]))

    ytail = {b: new_recv() for b in zblocks}
    last = [new_recv() for _ in range(8)]
    dest = (r, sib, mate)

    def finish(b):
        p, h, when = b // 2, b % 2, held(b, z)
        g = 2 * x + h
        here, away = x == dest[p], x != dest[p]
        if when is not None:
            here, away = here & when, away & when

        def flip():
            ft[b] = (tt[b, z] * scale).T

        only(turned(b), flip)
        for k in range(1, NY):
            rows = pl.ds(pl.multiple_of(((y + k) % NY) * 32, 32), 32)
            send(ft.at[b, rows], yt.at[zblocks.index(b), k - 1], ytail[b], at_y(k), turned(b), (b, 21, yt.at[zblocks.index(b)]))

        def keep():
            fr[b] = tt[b, z] * scale

        only(when, keep)
        for k in range(NY):
            yy = (y + k) % NY
            rows = pl.ds(pl.multiple_of(yy * 32, 32), 32)
            if k == 0:
                @pl.when(here)
                def _():
                    acc[g, y] = fr[b, rows]
            send(fr.at[b, rows], acc.at[g, y], last[0] + g, (z * NY + yy, r, dest[p]), when if k else away,
                 (b, 22, yt.at[zblocks.index(b)]) if k else None)

    def settle(b):
        p, g = b // 2, 2 * x + b % 2

        def act():
            i = zblocks.index(b)
            arrived(yt.at[i], ytail[b])
            fs[b] = (ft[b, own_y] + yt[i, 0]) + (yt[i, 1] + yt[i, 2])

        only(turned(b), act)
        send(fs.at[b], acc.at[z, 0], last[0] + z, (g * NY + y, dest[p], r), turned(b))

    lane = lax.broadcasted_iota(jnp.int32, (8, 128), 1) // 32

    def close(b):
        g = 2 * x + b % 2

        def act():
            v = tt[b, z, own_y]
            arrived(zt.at[b - 2], ztail[b])
            for k in range(1, NZ):
                v = v + zt[b - 2, k - 1]
            v = v * scale
            fs[b] = v
            turn = jnp.concatenate([v, jnp.zeros((96, 128), F32)], axis=0).T
            for q in range(4):
                w = jnp.zeros((8, 128), F32)
                for i in range(4):
                    rows = turn[q * 32 + i * 8:q * 32 + i * 8 + 8]
                    w = jnp.where(lane == i, pltpu.roll(rows, i * 32, 1) if i else rows, w)
                tp[b - 2, q] = w

        only(even, act)
        for q in range(4):
            send(tp.at[b - 2, q], tr.at[d], last[0] + z, (4 * g + q, sib, r), even, (b, 23, tp.at[b - 2]))

        @pl.when(even & (x == sib))
        def _():
            acc[g, 0] = fs[b]

        send(fs.at[b], acc.at[g, 0], last[0] + g, at_x(sib), even & (x != sib))

    own_tile, shared, cross = (0, 1), (2, 3), (4, 5)
    gram(0, khi[mine], klo[mine])
    zsend(own_tile)
    only(even, lambda: received(0))
    ysend(shared)
    zstep(own_tile, 0)
    received(1)
    zsend(cross)
    zstep(own_tile, 1)
    zstep(cross, 0)
    ystep(shared, 0)
    zstep(own_tile, 2)
    zstep(cross, 1)
    ystep(shared, 1)
    zstep(own_tile, 3)
    zstep(cross, 2)
    zstep(cross, 3)
    for b in own_tile:
        settle(b)
    for b in (2, 3):
        close(b)
    for b in (4, 5):
        settle(b)

    for g in range(8):
        mirrored = (x == user) | ((x == r) & ((z + NZ - g) % NZ >= 5))
        plain = ((x == r) & ((z + NZ - g) % NZ <= 4)) | (x == mate)
        cols = slice(g * 128, (g + 1) * 128)

        @pl.when(mirrored)
        def _():
            arrived(acc.at[g, 0], last[g])
            out_ref[:, cols] = acc[g, 0]

        @pl.when(plain)
        def _():
            @pl.when(x != g // 2)
            def _():
                arrived(acc.at[g], last[g])

            @pl.when(x == g // 2)
            def _():
                arrived(acc.at[g, 0:3], last[g])

            out_ref[:, cols] = (acc[g, 0] + acc[g, 1]) + (acc[g, 2] + acc[g, 3])

        @pl.when((x == sib) & even)
        def _():
            @pl.when(x != g // 2)
            def _():
                arrived(acc.at[g, 0], last[g])

            out_ref[:, cols] = acc[g, 0]

        @pl.when((x == sib) & jnp.logical_not(even))
        def _():
            arrived(tr.at[4 * g:4 * g + 4], last[g])
            for q in range(4):
                v = jnp.zeros((8, 128), F32)
                for i in range(NY):
                    rows = tr[g * NY + i]
                    turn = ((i - q) * 32) % 128
                    v = jnp.where(lane == i, pltpu.roll(rows, turn, 1) if turn else rows, v)
                out_ref[q * 8:q * 8 + 8, cols] = v

    for when, act in sends:
        only(when, act)


def per_device(total, env_desc, sparse_desc):
    vm = pltpu.VMEM
    width = env_desc.shape[1]
    return pl.pallas_call(
        functools.partial(body, 1.0 / total),
        out_shape=jax.ShapeDtypeStruct((32, PTS), F32),
        in_specs=[pl.BlockSpec(memory_space=pl.ANY)] * 2,
        out_specs=pl.BlockSpec(memory_space=pltpu.VMEM),
        scratch_shapes=[
            vm((PTS, width), F32), vm((PTS, width), BF16), vm((PTS, width), BF16),
            vm((4, ENV, width), F32), vm((2 * ENV, width), BF16),
            vm((4, PTS, ENV), F32), vm((PTS, 4 * ENV), BF16), vm((PTS, 4 * ENV), BF16),
            vm((2, 4, BLK, ENV), F32),
            vm((2, BLK, 4 * ENV), BF16), vm((2, BLK, 4 * ENV), BF16),
            vm((6, NZ, 128, 128), F32),
            vm((4, 4, 128, 128), F32), vm((4, 3, 128, 128), F32),
            vm((2, 2, NZ, 32, 128), F32), vm((2, NZ, 32, 128), F32), vm((2, NZ - 1, 32, 128), F32),
            vm((6, 128, 128), F32), vm((6, 128, 128), F32), vm((6, 32, 128), F32),
            vm((4, NY - 1, 32, 128), F32), vm((8, NY, 32, 128), F32),
            vm((2, 4, 8, 128), F32), vm((NZ * NY, 8, 128), F32),
            pltpu.SemaphoreType.DMA((5,)),
            pltpu.SemaphoreType.DMA((66,)),
            pltpu.SemaphoreType.DMA((96,)),
        ],
        compiler_params=pltpu.CompilerParams(
            collective_id=0, has_side_effects=True, vmem_limit_bytes=60 * 2 ** 20),
        cost_estimate=pl.CostEstimate(
            flops=6 * 4 * ENV * PTS * (width + 768), bytes_accessed=5 * 2 ** 20, transcendentals=0),
    )(env_desc, sparse_desc)


def solution(mesh):
    total = ENV * mesh.shape["depth"] * mesh.shape["col"]
    return jax.shard_map(
        functools.partial(per_device, total),
        mesh=mesh,
        in_specs=(P(("depth", "col"), None), P("row", None)),
        out_specs=P(("row", "depth"), "col"),
        check_vma=False,
    )
```

```python
import functools

import jax
import jax.numpy as jnp
from jax import lax
from jax.experimental import pallas as pl
from jax.experimental.pallas import tpu as pltpu
from jax.sharding import PartitionSpec as P

MESH = pl.DeviceIdType.MESH
NZ, NY, NX = 8, 4, 4
ENV = 128
PTS = 1024
BLK = 256
NT = (((1,), (1,)), ((), ()))
F32, BF16 = jnp.float32, jnp.bfloat16


def nt(a, b):
    return lax.dot_general(a, b, NT, preferred_element_type=F32)


def halves(v):
    hi = v.astype(BF16)
    return hi, (v - hi.astype(F32)).astype(BF16)


def body(scale, env_ref, sp_ref, out_ref, sf, shi, slo, eg, ec, kf, khi, klo, kx,
         jhi, jlo, tt, zn, zf, yn, yf, zt, fr, ft, fs, yt, acc, tp, tr, loc, ssem, rsem):
    d, r, x = lax.axis_index("depth"), lax.axis_index("row"), lax.axis_index("col")
    z, y, core, yl = d // NY, d % NY, r % 2, r // 2
    sib = r + 1 - 2 * core
    mate = (r + 2) * (1 - yl) + (3 - r) * yl
    user = (3 - r) * (1 - yl) + (r - 2) * yl
    right, left = (x + 1) % NX, (x + NX - 1) % NX

    def at_x(c):
        return (d, r, c)

    def at_row(q):
        return (d, q, x)

    def at_z(k):
        return (((z + k) % NZ) * NY + y, r, x)

    def at_y(k):
        return (z * NY + (y + k) % NY, r, x)

    count = [0, 0]
    sends = []

    def new_recv():
        count[1] += 1
        return count[1] - 1

    groups = {}

    def send(src, dst, to, dev, when=None, group=None):
        sem = count[0] if group is None else groups.get(group[:2], count[0])
        c = pltpu.make_async_remote_copy(
            src_ref=src, dst_ref=dst, send_sem=ssem.at[sem],
            recv_sem=rsem.at[to], device_id=dev, device_id_type=MESH)
        if sem == count[0]:
            count[0] += 1
            if group is None:
                sends.append((when, c.wait_send))
            else:
                groups[group[:2]] = sem
                sends.append((when, pltpu.make_async_copy(group[2], group[2], ssem.at[sem]).wait))
        only(when, c.start)

    def only(when, act):
        if when is None:
            act()
        else:
            pl.when(when)(act)

    def arrived(ref, sem):
        pltpu.make_async_copy(ref, ref, rsem.at[sem]).wait()

    load_e = pltpu.make_async_copy(env_ref, eg.at[0], loc.at[0])
    load_e.start()
    loads = []
    for i in range(4):
        rows = pl.ds(i * 256, 256)
        c = pltpu.make_async_copy(sp_ref.at[rows], sf.at[rows], loc.at[1 + i])
        c.start()
        loads.append(c)

    bar = pltpu.get_barrier_semaphore()

    def greet(dev):
        pl.semaphore_signal(bar, inc=1, device_id=dev, device_id_type=MESH)

    greet(at_x(left))
    greet(at_x(right))
    greet(at_row(sib))
    greet(at_row(mate))
    for k in range(1, NZ):
        greet(at_z(k))
    for k in range(1, NY):
        greet(at_y(k))
    pl.semaphore_wait(bar, 14)

    def piece(side, half, p):
        if side == 3:
            return eg.at[3, pl.ds(pl.multiple_of(half * 64 + p * 32, 32), 32)]
        slot = 1 if side == 1 + p else 2
        return eg.at[slot, pl.ds(pl.multiple_of(half * 32 + (side - 1) * 64, 32), 32)]

    def own(p):
        return env_ref.at[pl.ds(pl.multiple_of(core * 64 + p * 32, 32), 32)]

    ring = {(s, p): new_recv() for s in (1, 2, 3) for p in (0, 1)}
    pair = {(s, p): new_recv() for s in (1, 2, 3) for p in (0, 1)}
    send(own(0), piece(1, core, 0), ring[1, 0], at_x(right))
    send(own(1), piece(2, core, 1), ring[2, 1], at_x(left))
    send(own(1), piece(1, core, 1), ring[1, 1], at_x(right))
    send(own(0), piece(2, core, 0), ring[2, 0], at_x(left))

    def to_sib(s, p):
        send(piece(s, core, p), piece(s, core, p), pair[s, p], at_row(sib))

    for i in range(4):
        loads[i].wait()

        @pl.loop(0, 4)
        def _(j):
            rows = pl.ds(pl.multiple_of(i * 256 + j * 64, 64), 64)
            hi, lo = halves(sf[rows])
            shi[rows] = hi
            slo[rows] = lo

    load_e.wait()

    mine = pl.ds(pl.multiple_of(x * BLK, BLK), BLK)
    krecv = {(w, s): new_recv() for w in (0, 1) for s in range(4)}

    def shard(s):
        hi, lo = halves(eg[s])
        ec[0:ENV] = hi
        ec[ENV:] = lo
        cols = slice(s * ENV, (s + 1) * ENV)

        def some(i, c):
            rows = pl.ds(pl.multiple_of(((x + i) % 4) * 256, 256), 256)
            both = nt(shi[rows], ec[...])
            low = nt(slo[rows], ec[0:ENV])
            dots = both[:, :ENV] + (both[:, ENV:] + low)
            sq = dots * dots
            k = sq * sq
            kf[s, rows] = k
            a, b = halves(k)
            khi[rows, cols] = a
            klo[rows, cols] = b
            return c

        some(0, 0)
        send(kf.at[s, mine], kx.at[1, s], krecv[1, s], at_row(user))
        send(kf.at[s, mine], kx.at[0, s], krecv[0, s], at_row(sib), core == 1)
        lax.fori_loop(1, 4, some, 0)

    shard(0)
    arrived(piece(1, core, 0), ring[1, 0])
    send(piece(1, core, 0), piece(3, core, 0), ring[3, 0], at_x(right))
    to_sib(1, 0)
    arrived(piece(2, core, 1), ring[2, 1])
    send(piece(2, core, 1), piece(3, core, 1), ring[3, 1], at_x(left))
    to_sib(2, 1)
    arrived(piece(1, 1 - core, 0), pair[1, 0])
    arrived(piece(2, 1 - core, 1), pair[2, 1])
    shard(1)
    for side, p in ((1, 1), (2, 0)):
        arrived(piece(side, core, p), ring[side, p])
        to_sib(side, p)
    for side, p in ((1, 1), (2, 0)):
        arrived(piece(side, 1 - core, p), pair[side, p])
    shard(2)
    for p in (0, 1):
        arrived(piece(3, core, p), ring[3, p])
        to_sib(3, p)
    for p in (0, 1):
        arrived(piece(3, 1 - core, p), pair[3, p])
    shard(3)

    even = core == 0
    zblocks, yblocks = (0, 1, 4, 5), (2, 3)
    near = {(b, t, u): new_recv() for b in zblocks for t in range(4) for u in range(2)}
    far = {(b, t, u): new_recv() for b in zblocks for t in range(3) for u in range(2)}
    ynear = {(b, t, v): new_recv() for b in yblocks for t in range(2) for v in range(2)}
    yfar = {b: new_recv() for b in yblocks}
    ztail = {b: new_recv() for b in yblocks}

    def gram(p, rhi, rlo):
        @pl.loop(0, 4)
        def _(i):
            rows = pl.ds(pl.multiple_of(i * 256, 256), 256)
            a = khi[rows]
            g = nt(a, rhi) + (nt(a, rlo) + nt(klo[rows], rhi))
            for h in range(2):
                for q in range(2):
                    tt[2 * p + h, 2 * i + q] = g[q * 128:(q + 1) * 128, h * 128:(h + 1) * 128]

    def received(w):
        for s in range(4):
            arrived(kx.at[w, s], krecv[w, s])
            hi, lo = halves(kx[w, s])
            jhi[w, :, s * ENV:(s + 1) * ENV] = hi
            jlo[w, :, s * ENV:(s + 1) * ENV] = lo
        gram(1 + w, jhi[w], jlo[w])

    def gap(b, c):
        return (c + 2 * NZ - 2 * x - b % 2) % NZ

    def held(b, c):
        return (gap(b, c) <= 4, even, None)[b // 2]

    def turned(b):
        return ((gap(b, z) >= 1) & (gap(b, z) <= 3), even, None)[b // 2]

    def half(u):
        return pl.ds(u * 64, 64)

    def znear(b, t, u):
        m = 1 - 2 * (b % 2)
        c = (z + NZ + m * (4 - t)) % NZ
        send(tt.at[b, c, half(u)], zn.at[zblocks.index(b), t, half(u)], near[b, t, u], at_z(m % NZ), held(b, c),
             (b, t, zn.at[zblocks.index(b), t]) if b < 2 else (b, 4, zn.at[zblocks.index(b)]))

    def zfar(b, t, u):
        m = 1 - 2 * (b % 2)
        c = (z + NZ - m * (3 - t)) % NZ
        send(tt.at[b, c, half(u)], zf.at[zblocks.index(b), t, half(u)], far[b, t, u], at_z(-m % NZ), held(b, c),
             (b, 8 + t, zf.at[zblocks.index(b), t]) if b < 2 else (b, 12, zf.at[zblocks.index(b)]))

    def zsend(blocks):
        for f in (znear, zfar):
            for u in range(2):
                for b in blocks:
                    f(b, 0, u)

    def zstep(blocks, t):
        def take(b, c, u, slot, sem):
            def act():
                arrived(slot, sem)
                tt[b, c, half(u)] = tt[b, c, half(u)] + slot[...]
            only(held(b, c), act)

        for u in range(2):
            for b in blocks:
                m = 1 - 2 * (b % 2)
                take(b, (z + NZ + m * (3 - t)) % NZ, u, zn.at[zblocks.index(b), t, half(u)], near[b, t, u])
                if t < 3:
                    znear(b, t + 1, u)
                elif u == 1:
                    finish(b)
        if t < 3:
            for u in range(2):
                for b in blocks:
                    m = 1 - 2 * (b % 2)
                    take(b, (z + NZ - m * (2 - t)) % NZ, u, zf.at[zblocks.index(b), t, half(u)], far[b, t, u])
                    if t < 2:
                        zfar(b, t + 1, u)

    own_y = pl.ds(pl.multiple_of(y * 32, 32), 32)

    def ychunk(k):
        return pl.ds(pl.multiple_of(((y + k) % NY) * 32, 32), 32)

    def four(v):
        return pl.ds(v * 4, 4)

    def ynext(b, t, v):
        m = 1 - 2 * (b % 2)
        send(tt.at[b, four(v), ychunk((2 - t) * m % NY)], yn.at[b - 2, t, four(v)], ynear[b, t, v], at_y(m % NY), even)

    def ysend(blocks):
        for v in range(2):
            for b in blocks:
                ynext(b, 0, v)
        for b in blocks:
            m = 1 - 2 * (b % 2)
            send(tt.at[b, :, ychunk(-m % NY)], yf.at[b - 2], yfar[b], at_y(-m % NY), even)

    def ystep(blocks, t):
        for v in range(2):
            for b in blocks:
                m = 1 - 2 * (b % 2)
                c = ychunk((1 - t) * m % NY)

                def act():
                    arrived(yn.at[b - 2, t, four(v)], ynear[b, t, v])
                    if t == 1 and v == 0:
                        arrived(yf.at[b - 2], yfar[b])
                    w = tt[b, four(v), c] + yn[b - 2, t, four(v)]
                    tt[b, four(v), c] = w if t == 0 else w + yf[b - 2, four(v)]

                only(even, act)
                if t == 0:
                    ynext(b, 1, v)
        for b in blocks:
            if t == 1:
                for k in range(1, NZ):
                    send(tt.at[b, (z + k) % NZ, own_y], zt.at[b - 2, k - 1], ztail[b], at_z(k), even, (b, 20, zt.at[b - 2]))

    ytail = {b: new_recv() for b in zblocks}
    last = [new_recv() for _ in range(8)]
    dest = (r, sib, mate)

    def finish(b):
        p, h, when = b // 2, b % 2, held(b, z)
        g = 2 * x + h
        here, away = x == dest[p], x != dest[p]
        if when is not None:
            here, away = here & when, away & when

        def flip():
            ft[b] = (tt[b, z] * scale).T

        only(turned(b), flip)
        for k in range(1, NY):
            rows = pl.ds(pl.multiple_of(((y + k) % NY) * 32, 32), 32)
            send(ft.at[b, rows], yt.at[zblocks.index(b), k - 1], ytail[b], at_y(k), turned(b), (b, 21, yt.at[zblocks.index(b)]))

        def keep():
            fr[b] = tt[b, z] * scale

        only(when, keep)
        for k in range(NY):
            yy = (y + k) % NY
            rows = pl.ds(pl.multiple_of(yy * 32, 32), 32)
            if k == 0:
                @pl.when(here)
                def _():
                    acc[g, y] = fr[b, rows]
            send(fr.at[b, rows], acc.at[g, y], last[0] + g, (z * NY + yy, r, dest[p]), when if k else away,
                 (b, 22, yt.at[zblocks.index(b)]) if k else None)

    def settle(b):
        p, g = b // 2, 2 * x + b % 2

        def act():
            i = zblocks.index(b)
            arrived(yt.at[i], ytail[b])
            fs[b] = (ft[b, own_y] + yt[i, 0]) + (yt[i, 1] + yt[i, 2])

        only(turned(b), act)
        send(fs.at[b], acc.at[z, 0], last[0] + z, (g * NY + y, dest[p], r), turned(b))

    lane = lax.broadcasted_iota(jnp.int32, (8, 128), 1) // 32

    def close(b):
        g = 2 * x + b % 2

        def act():
            v = tt[b, z, own_y]
            arrived(zt.at[b - 2], ztail[b])
            for k in range(1, NZ):
                v = v + zt[b - 2, k - 1]
            v = v * scale
            fs[b] = v
            turn = jnp.concatenate([v, jnp.zeros((96, 128), F32)], axis=0).T
            for q in range(4):
                w = jnp.zeros((8, 128), F32)
                for i in range(4):
                    rows = turn[q * 32 + i * 8:q * 32 + i * 8 + 8]
                    w = jnp.where(lane == i, pltpu.roll(rows, i * 32, 1) if i else rows, w)
                tp[b - 2, q] = w

        only(even, act)
        for q in range(4):
            send(tp.at[b - 2, q], tr.at[d], last[0] + z, (4 * g + q, sib, r), even, (b, 23, tp.at[b - 2]))

        @pl.when(even & (x == sib))
        def _():
            acc[g, 0] = fs[b]

        send(fs.at[b], acc.at[g, 0], last[0] + g, at_x(sib), even & (x != sib))

    own_tile, shared, cross = (0, 1), (2, 3), (4, 5)
    gram(0, khi[mine], klo[mine])
    zsend(own_tile)
    only(even, lambda: received(0))
    ysend(shared)
    zstep(own_tile, 0)
    received(1)
    zsend(cross)
    zstep(own_tile, 1)
    zstep(cross, 0)
    ystep(shared, 0)
    zstep(own_tile, 2)
    zstep(cross, 1)
    ystep(shared, 1)
    zstep(own_tile, 3)
    zstep(cross, 2)
    zstep(cross, 3)
    for b in own_tile:
        settle(b)
    for b in (2, 3):
        close(b)
    for b in (4, 5):
        settle(b)

    for g in range(8):
        mirrored = (x == user) | ((x == r) & ((z + NZ - g) % NZ >= 5))
        plain = ((x == r) & ((z + NZ - g) % NZ <= 4)) | (x == mate)
        cols = slice(g * 128, (g + 1) * 128)

        @pl.when(mirrored)
        def _():
            arrived(acc.at[g, 0], last[g])
            out_ref[:, cols] = acc[g, 0]

        @pl.when(plain)
        def _():
            @pl.when(x != g // 2)
            def _():
                arrived(acc.at[g], last[g])

            @pl.when(x == g // 2)
            def _():
                arrived(acc.at[g, 0:3], last[g])

            out_ref[:, cols] = (acc[g, 0] + acc[g, 1]) + (acc[g, 2] + acc[g, 3])

        @pl.when((x == sib) & even)
        def _():
            @pl.when(x != g // 2)
            def _():
                arrived(acc.at[g, 0], last[g])

            out_ref[:, cols] = acc[g, 0]

        @pl.when((x == sib) & jnp.logical_not(even))
        def _():
            arrived(tr.at[4 * g:4 * g + 4], last[g])
            for q in range(4):
                v = jnp.zeros((8, 128), F32)
                for i in range(NY):
                    rows = tr[g * NY + i]
                    turn = ((i - q) * 32) % 128
                    v = jnp.where(lane == i, pltpu.roll(rows, turn, 1) if turn else rows, v)
                out_ref[q * 8:q * 8 + 8, cols] = v

    for when, act in sends:
        only(when, act)


def per_device(total, env_desc, sparse_desc):
    vm = pltpu.VMEM
    width = env_desc.shape[1]
    return pl.pallas_call(
        functools.partial(body, 1.0 / total),
        out_shape=jax.ShapeDtypeStruct((32, PTS), F32),
        in_specs=[pl.BlockSpec(memory_space=pl.ANY)] * 2,
        out_specs=pl.BlockSpec(memory_space=pltpu.VMEM),
        scratch_shapes=[
            vm((PTS, width), F32), vm((PTS, width), BF16), vm((PTS, width), BF16),
            vm((4, ENV, width), F32), vm((2 * ENV, width), BF16),
            vm((4, PTS, ENV), F32), vm((PTS, 4 * ENV), BF16), vm((PTS, 4 * ENV), BF16),
            vm((2, 4, BLK, ENV), F32),
            vm((2, BLK, 4 * ENV), BF16), vm((2, BLK, 4 * ENV), BF16),
            vm((6, NZ, 128, 128), F32),
            vm((4, 4, 128, 128), F32), vm((4, 3, 128, 128), F32),
            vm((2, 2, NZ, 32, 128), F32), vm((2, NZ, 32, 128), F32), vm((2, NZ - 1, 32, 128), F32),
            vm((6, 128, 128), F32), vm((6, 128, 128), F32), vm((6, 32, 128), F32),
            vm((4, NY - 1, 32, 128), F32), vm((8, NY, 32, 128), F32),
            vm((2, 4, 8, 128), F32), vm((NZ * NY, 8, 128), F32),
            pltpu.SemaphoreType.DMA((5,)),
            pltpu.SemaphoreType.DMA((70,)),
            pltpu.SemaphoreType.DMA((100,)),
        ],
        compiler_params=pltpu.CompilerParams(
            collective_id=0, has_side_effects=True, vmem_limit_bytes=52 * 2 ** 20),
        cost_estimate=pl.CostEstimate(
            flops=6 * 4 * ENV * PTS * (width + 768), bytes_accessed=5 * 2 ** 20, transcendentals=0),
    )(env_desc, sparse_desc)


def solution(mesh):
    total = ENV * mesh.shape["depth"] * mesh.shape["col"]
    return jax.shard_map(
        functools.partial(per_device, total),
        mesh=mesh,
        in_specs=(P(("depth", "col"), None), P("row", None)),
        out_specs=P(("row", "depth"), "col"),
        check_vma=False,
    )
```

```python
import functools

import jax
import jax.numpy as jnp
from jax import lax
from jax.experimental import pallas as pl
from jax.experimental.pallas import tpu as pltpu
from jax.sharding import PartitionSpec as P

MESH = pl.DeviceIdType.MESH
NZ, NY, NX = 8, 4, 4
ENV = 128
PTS = 1024
BLK = 256
NT = (((1,), (1,)), ((), ()))
F32, BF16 = jnp.float32, jnp.bfloat16


def nt(a, b):
    return lax.dot_general(a, b, NT, preferred_element_type=F32)


def halves(v):
    hi = v.astype(BF16)
    return hi, (v - hi.astype(F32)).astype(BF16)


def body(scale, env_ref, sp_ref, out_ref, sf, shi, slo, eg, ec, kf, khi, klo, kx,
         jhi, jlo, tt, zn, zf, yn, yf, zt, fr, ft, fs, yt, acc, tp, tr, loc, ssem, rsem):
    d, r, x = lax.axis_index("depth"), lax.axis_index("row"), lax.axis_index("col")
    z, y, core, yl = d // NY, d % NY, r % 2, r // 2
    sib = r + 1 - 2 * core
    mate = (r + 2) * (1 - yl) + (3 - r) * yl
    user = (3 - r) * (1 - yl) + (r - 2) * yl
    right, left = (x + 1) % NX, (x + NX - 1) % NX

    def at_x(c):
        return (d, r, c)

    def at_row(q):
        return (d, q, x)

    def at_z(k):
        return (((z + k) % NZ) * NY + y, r, x)

    def at_y(k):
        return (z * NY + (y + k) % NY, r, x)

    count = [0, 0]
    sends = []

    def new_recv():
        count[1] += 1
        return count[1] - 1

    groups = {}

    def send(src, dst, to, dev, when=None, group=None):
        sem = count[0] if group is None else groups.get(group[:2], count[0])
        c = pltpu.make_async_remote_copy(
            src_ref=src, dst_ref=dst, send_sem=ssem.at[sem],
            recv_sem=rsem.at[to], device_id=dev, device_id_type=MESH)
        if sem == count[0]:
            count[0] += 1
            if group is None:
                sends.append((when, c.wait_send))
            else:
                groups[group[:2]] = sem
                sends.append((when, pltpu.make_async_copy(group[2], group[2], ssem.at[sem]).wait))
        only(when, c.start)

    def only(when, act):
        if when is None:
            act()
        else:
            pl.when(when)(act)

    def arrived(ref, sem):
        pltpu.make_async_copy(ref, ref, rsem.at[sem]).wait()

    load_e = pltpu.make_async_copy(env_ref, eg.at[0], loc.at[0])
    load_e.start()
    loads = []
    for i in range(4):
        rows = pl.ds(i * 256, 256)
        c = pltpu.make_async_copy(sp_ref.at[rows], sf.at[rows], loc.at[1 + i])
        c.start()
        loads.append(c)

    bar = pltpu.get_barrier_semaphore()

    def greet(dev):
        pl.semaphore_signal(bar, inc=1, device_id=dev, device_id_type=MESH)

    greet(at_x(left))
    greet(at_x(right))
    greet(at_row(sib))
    greet(at_row(mate))
    for k in range(1, NZ):
        greet(at_z(k))
    for k in range(1, NY):
        greet(at_y(k))
    pl.semaphore_wait(bar, 14)

    def piece(side, half, p):
        if side == 3:
            return eg.at[3, pl.ds(pl.multiple_of(half * 64 + p * 32, 32), 32)]
        slot = 1 if side == 1 + p else 2
        return eg.at[slot, pl.ds(pl.multiple_of(half * 32 + (side - 1) * 64, 32), 32)]

    def own(p):
        return env_ref.at[pl.ds(pl.multiple_of(core * 64 + p * 32, 32), 32)]

    ring = {(s, p): new_recv() for s in (1, 2, 3) for p in (0, 1)}
    pair = {(s, p): new_recv() for s in (1, 2, 3) for p in (0, 1)}
    send(own(0), piece(1, core, 0), ring[1, 0], at_x(right))
    send(own(1), piece(2, core, 1), ring[2, 1], at_x(left))
    send(own(1), piece(1, core, 1), ring[1, 1], at_x(right))
    send(own(0), piece(2, core, 0), ring[2, 0], at_x(left))

    def to_sib(s, p):
        send(piece(s, core, p), piece(s, core, p), pair[s, p], at_row(sib))

    for i in range(4):
        loads[i].wait()

        @pl.loop(0, 4)
        def _(j):
            rows = pl.ds(pl.multiple_of(i * 256 + j * 64, 64), 64)
            hi, lo = halves(sf[rows])
            shi[rows] = hi
            slo[rows] = lo

    load_e.wait()

    mine = pl.ds(pl.multiple_of(x * BLK, BLK), BLK)
    krecv = {(w, s): new_recv() for w in (0, 1) for s in range(4)}

    def shard(s):
        hi, lo = halves(eg[s])
        ec[0:ENV] = hi
        ec[ENV:] = lo
        cols = slice(s * ENV, (s + 1) * ENV)

        def some(i, c):
            rows = pl.ds(pl.multiple_of(((x + i) % 4) * 256, 256), 256)
            both = nt(shi[rows], ec[...])
            low = nt(slo[rows], ec[0:ENV])
            dots = both[:, :ENV] + (both[:, ENV:] + low)
            sq = dots * dots
            k = sq * sq
            kf[s, rows] = k
            a, b = halves(k)
            khi[rows, cols] = a
            klo[rows, cols] = b
            return c

        some(0, 0)
        send(kf.at[s, mine], kx.at[1, s], krecv[1, s], at_row(user))
        send(kf.at[s, mine], kx.at[0, s], krecv[0, s], at_row(sib), core == 1)
        lax.fori_loop(1, 4, some, 0)

    shard(0)
    arrived(piece(1, core, 0), ring[1, 0])
    send(piece(1, core, 0), piece(3, core, 0), ring[3, 0], at_x(right))
    to_sib(1, 0)
    arrived(piece(2, core, 1), ring[2, 1])
    send(piece(2, core, 1), piece(3, core, 1), ring[3, 1], at_x(left))
    to_sib(2, 1)
    arrived(piece(1, 1 - core, 0), pair[1, 0])
    arrived(piece(2, 1 - core, 1), pair[2, 1])
    shard(1)
    for side, p in ((1, 1), (2, 0)):
        arrived(piece(side, core, p), ring[side, p])
        to_sib(side, p)
    for side, p in ((1, 1), (2, 0)):
        arrived(piece(side, 1 - core, p), pair[side, p])
    shard(2)
    for p in (0, 1):
        arrived(piece(3, core, p), ring[3, p])
        to_sib(3, p)
    for p in (0, 1):
        arrived(piece(3, 1 - core, p), pair[3, p])
    shard(3)

    even = core == 0
    zblocks, yblocks = (0, 1, 4, 5), (2, 3)
    near = {(b, t, u): new_recv() for b in zblocks for t in range(4) for u in range(2)}
    far = {(b, t, u): new_recv() for b in zblocks for t in range(3) for u in range(2)}
    ynear = {(b, t, v): new_recv() for b in yblocks for t in range(2) for v in range(2)}
    yfar = {b: new_recv() for b in yblocks}
    ztail = {b: new_recv() for b in yblocks}

    def gram(p, rhi, rlo):
        @pl.loop(0, 4)
        def _(i):
            rows = pl.ds(pl.multiple_of(i * 256, 256), 256)
            a = khi[rows]
            g = nt(a, rhi) + (nt(a, rlo) + nt(klo[rows], rhi))
            for h in range(2):
                for q in range(2):
                    tt[2 * p + h, 2 * i + q] = g[q * 128:(q + 1) * 128, h * 128:(h + 1) * 128]

    def received(w, shards):
        for s in shards:
            arrived(kx.at[w, s], krecv[w, s])
            hi, lo = halves(kx[w, s])
            jhi[w, :, s * ENV:(s + 1) * ENV] = hi
            jlo[w, :, s * ENV:(s + 1) * ENV] = lo
        if shards[-1] < 3:
            return
        gram(1 + w, jhi[w], jlo[w])

    def gap(b, c):
        return (c + 2 * NZ - 2 * x - b % 2) % NZ

    def held(b, c):
        return (gap(b, c) <= 4, even, None)[b // 2]

    def turned(b):
        return ((gap(b, z) >= 1) & (gap(b, z) <= 3), even, None)[b // 2]

    def half(u):
        return pl.ds(u * 64, 64)

    def znear(b, t, u):
        m = 1 - 2 * (b % 2)
        c = (z + NZ + m * (4 - t)) % NZ
        send(tt.at[b, c, half(u)], zn.at[zblocks.index(b), t, half(u)], near[b, t, u], at_z(m % NZ), held(b, c),
             (b, t, zn.at[zblocks.index(b), t]) if b < 2 else (b, 4, zn.at[zblocks.index(b)]))

    def zfar(b, t, u):
        m = 1 - 2 * (b % 2)
        c = (z + NZ - m * (3 - t)) % NZ
        send(tt.at[b, c, half(u)], zf.at[zblocks.index(b), t, half(u)], far[b, t, u], at_z(-m % NZ), held(b, c),
             (b, 8 + t, zf.at[zblocks.index(b), t]) if b < 2 else (b, 12, zf.at[zblocks.index(b)]))

    def zsend(blocks):
        for f in (znear, zfar):
            for u in range(2):
                for b in blocks:
                    f(b, 0, u)

    def zstep(blocks, t):
        def take(b, c, u, slot, sem):
            def act():
                arrived(slot, sem)
                tt[b, c, half(u)] = tt[b, c, half(u)] + slot[...]
            only(held(b, c), act)

        for u in range(2):
            for b in blocks:
                m = 1 - 2 * (b % 2)
                take(b, (z + NZ + m * (3 - t)) % NZ, u, zn.at[zblocks.index(b), t, half(u)], near[b, t, u])
                if t < 3:
                    znear(b, t + 1, u)
                elif u == 1:
                    finish(b)
        if t < 3:
            for u in range(2):
                for b in blocks:
                    m = 1 - 2 * (b % 2)
                    take(b, (z + NZ - m * (2 - t)) % NZ, u, zf.at[zblocks.index(b), t, half(u)], far[b, t, u])
                    if t < 2:
                        zfar(b, t + 1, u)

    own_y = pl.ds(pl.multiple_of(y * 32, 32), 32)

    def ychunk(k):
        return pl.ds(pl.multiple_of(((y + k) % NY) * 32, 32), 32)

    def four(v):
        return pl.ds(v * 4, 4)

    def ynext(b, t, v):
        m = 1 - 2 * (b % 2)
        send(tt.at[b, four(v), ychunk((2 - t) * m % NY)], yn.at[b - 2, t, four(v)], ynear[b, t, v], at_y(m % NY), even)

    def ysend(blocks):
        for v in range(2):
            for b in blocks:
                ynext(b, 0, v)
        for b in blocks:
            m = 1 - 2 * (b % 2)
            send(tt.at[b, :, ychunk(-m % NY)], yf.at[b - 2], yfar[b], at_y(-m % NY), even)

    def ystep(blocks, t):
        for v in range(2):
            for b in blocks:
                m = 1 - 2 * (b % 2)
                c = ychunk((1 - t) * m % NY)

                def act():
                    arrived(yn.at[b - 2, t, four(v)], ynear[b, t, v])
                    if t == 1 and v == 0:
                        arrived(yf.at[b - 2], yfar[b])
                    w = tt[b, four(v), c] + yn[b - 2, t, four(v)]
                    tt[b, four(v), c] = w if t == 0 else w + yf[b - 2, four(v)]

                only(even, act)
                if t == 0:
                    ynext(b, 1, v)
        for b in blocks:
            if t == 1:
                for k in range(1, NZ):
                    send(tt.at[b, (z + k) % NZ, own_y], zt.at[b - 2, k - 1], ztail[b], at_z(k), even, (b, 20, zt.at[b - 2]))

    ytail = {b: new_recv() for b in zblocks}
    last = [new_recv() for _ in range(8)]
    dest = (r, sib, mate)

    def finish(b):
        p, h, when = b // 2, b % 2, held(b, z)
        g = 2 * x + h
        here, away = x == dest[p], x != dest[p]
        if when is not None:
            here, away = here & when, away & when

        def flip():
            ft[b] = (tt[b, z] * scale).T

        only(turned(b), flip)
        for k in range(1, NY):
            rows = pl.ds(pl.multiple_of(((y + k) % NY) * 32, 32), 32)
            send(ft.at[b, rows], yt.at[zblocks.index(b), k - 1], ytail[b], at_y(k), turned(b), (b, 21, yt.at[zblocks.index(b)]))

        def keep():
            fr[b] = tt[b, z] * scale

        only(when, keep)
        for k in range(NY):
            yy = (y + k) % NY
            rows = pl.ds(pl.multiple_of(yy * 32, 32), 32)
            if k == 0:
                @pl.when(here)
                def _():
                    acc[g, y] = fr[b, rows]
            send(fr.at[b, rows], acc.at[g, y], last[0] + g, (z * NY + yy, r, dest[p]), when if k else away,
                 (b, 22, yt.at[zblocks.index(b)]) if k else None)

    def settle(b):
        p, g = b // 2, 2 * x + b % 2

        def act():
            i = zblocks.index(b)
            arrived(yt.at[i], ytail[b])
            fs[b] = (ft[b, own_y] + yt[i, 0]) + (yt[i, 1] + yt[i, 2])

        only(turned(b), act)
        send(fs.at[b], acc.at[z, 0], last[0] + z, (g * NY + y, dest[p], r), turned(b))

    lane = lax.broadcasted_iota(jnp.int32, (8, 128), 1) // 32

    def close(b):
        g = 2 * x + b % 2

        def act():
            v = tt[b, z, own_y]
            arrived(zt.at[b - 2], ztail[b])
            for k in range(1, NZ):
                v = v + zt[b - 2, k - 1]
            v = v * scale
            fs[b] = v
            turn = jnp.concatenate([v, jnp.zeros((96, 128), F32)], axis=0).T
            for q in range(4):
                w = jnp.zeros((8, 128), F32)
                for i in range(4):
                    rows = turn[q * 32 + i * 8:q * 32 + i * 8 + 8]
                    w = jnp.where(lane == i, pltpu.roll(rows, i * 32, 1) if i else rows, w)
                tp[b - 2, q] = w

        only(even, act)
        for q in range(4):
            send(tp.at[b - 2, q], tr.at[d], last[0] + z, (4 * g + q, sib, r), even, (b, 23, tp.at[b - 2]))

        @pl.when(even & (x == sib))
        def _():
            acc[g, 0] = fs[b]

        send(fs.at[b], acc.at[g, 0], last[0] + g, at_x(sib), even & (x != sib))

    own_tile, shared, cross = (0, 1), (2, 3), (4, 5)
    gram(0, khi[mine], klo[mine])
    zsend(own_tile)
    only(even, lambda: received(0, (0, 1, 2, 3)))
    ysend(shared)
    received(1, (0, 1, 2))
    zstep(own_tile, 0)
    received(1, (3,))
    zsend(cross)
    zstep(own_tile, 1)
    zstep(cross, 0)
    ystep(shared, 0)
    zstep(own_tile, 2)
    zstep(cross, 1)
    ystep(shared, 1)
    zstep(own_tile, 3)
    zstep(cross, 2)
    zstep(cross, 3)
    for b in own_tile:
        settle(b)
    for b in (2, 3):
        close(b)
    for b in (4, 5):
        settle(b)

    for g in range(8):
        mirrored = (x == user) | ((x == r) & ((z + NZ - g) % NZ >= 5))
        plain = ((x == r) & ((z + NZ - g) % NZ <= 4)) | (x == mate)
        cols = slice(g * 128, (g + 1) * 128)

        @pl.when(mirrored)
        def _():
            arrived(acc.at[g, 0], last[g])
            out_ref[:, cols] = acc[g, 0]

        @pl.when(plain)
        def _():
            @pl.when(x != g // 2)
            def _():
                arrived(acc.at[g], last[g])

            @pl.when(x == g // 2)
            def _():
                arrived(acc.at[g, 0:3], last[g])

            out_ref[:, cols] = (acc[g, 0] + acc[g, 1]) + (acc[g, 2] + acc[g, 3])

        @pl.when((x == sib) & even)
        def _():
            @pl.when(x != g // 2)
            def _():
                arrived(acc.at[g, 0], last[g])

            out_ref[:, cols] = acc[g, 0]

        @pl.when((x == sib) & jnp.logical_not(even))
        def _():
            arrived(tr.at[4 * g:4 * g + 4], last[g])
            for q in range(4):
                v = jnp.zeros((8, 128), F32)
                for i in range(NY):
                    rows = tr[g * NY + i]
                    turn = ((i - q) * 32) % 128
                    v = jnp.where(lane == i, pltpu.roll(rows, turn, 1) if turn else rows, v)
                out_ref[q * 8:q * 8 + 8, cols] = v

    for when, act in sends:
        only(when, act)


def per_device(total, env_desc, sparse_desc):
    vm = pltpu.VMEM
    width = env_desc.shape[1]
    return pl.pallas_call(
        functools.partial(body, 1.0 / total),
        out_shape=jax.ShapeDtypeStruct((32, PTS), F32),
        in_specs=[pl.BlockSpec(memory_space=pl.ANY)] * 2,
        out_specs=pl.BlockSpec(memory_space=pltpu.VMEM),
        scratch_shapes=[
            vm((PTS, width), F32), vm((PTS, width), BF16), vm((PTS, width), BF16),
            vm((4, ENV, width), F32), vm((2 * ENV, width), BF16),
            vm((4, PTS, ENV), F32), vm((PTS, 4 * ENV), BF16), vm((PTS, 4 * ENV), BF16),
            vm((2, 4, BLK, ENV), F32),
            vm((2, BLK, 4 * ENV), BF16), vm((2, BLK, 4 * ENV), BF16),
            vm((6, NZ, 128, 128), F32),
            vm((4, 4, 128, 128), F32), vm((4, 3, 128, 128), F32),
            vm((2, 2, NZ, 32, 128), F32), vm((2, NZ, 32, 128), F32), vm((2, NZ - 1, 32, 128), F32),
            vm((6, 128, 128), F32), vm((6, 128, 128), F32), vm((6, 32, 128), F32),
            vm((4, NY - 1, 32, 128), F32), vm((8, NY, 32, 128), F32),
            vm((2, 4, 8, 128), F32), vm((NZ * NY, 8, 128), F32),
            pltpu.SemaphoreType.DMA((5,)),
            pltpu.SemaphoreType.DMA((70,)),
            pltpu.SemaphoreType.DMA((100,)),
        ],
        compiler_params=pltpu.CompilerParams(
            collective_id=0, has_side_effects=True, vmem_limit_bytes=52 * 2 ** 20),
        cost_estimate=pl.CostEstimate(
            flops=6 * 4 * ENV * PTS * (width + 768), bytes_accessed=5 * 2 ** 20, transcendentals=0),
    )(env_desc, sparse_desc)


def solution(mesh):
    total = ENV * mesh.shape["depth"] * mesh.shape["col"]
    return jax.shard_map(
        functools.partial(per_device, total),
        mesh=mesh,
        in_specs=(P(("depth", "col"), None), P("row", None)),
        out_specs=P(("row", "depth"), "col"),
        check_vma=False,
    )
```
